32 devices in a mesh: groups: 2 (over y), brow: 4 (over z), bcol: 2 (over x), mpo: 2 (over core).
Axes of the slice: x: 2, y: 2, z: 4, core: 2. Of those that a mesh axis runs over, the one named last changes fastest.
Arguments:
- amplitudes: bfloat16 [512, 16, 256], P(('groups', 'brow'), None, 'bcol'), parts along dimension 0, may hold values from -18 to 18
- left_env: bfloat16 [52, 256, 192], P(('groups', 'mpo'), 'brow'), parts along dimension 0, may hold values from -1 to 2
- right_env: bfloat16 [52, 256, 128], P('groups', 'bcol'), parts along dimension 0, may hold values from -1 to 2
- mpo_left: float32 [26, 26, 4, 4], replicated, may hold values from -1 to 1
- mpo_right: float32 [26, 26, 4, 4], replicated, may hold values from -1 to 1
- sector_table: int32 [512], P('groups'), parts along dimension 0, may hold values from 0 to 3, never falling along the last dimension, each value on 1 to 128 neighbouring positions
Outputs:
- image_two: bfloat16 [512, 16, 256], P(('groups', 'brow'), 'mpo', 'bcol'), parts along dimension 0
- basis_two: bfloat16 [512, 16, 256], P(('groups', 'brow'), 'mpo', 'bcol'), parts along dimension 0
- projected: float32 [4, 2], P('groups'), parts along dimension 0
The draws below stay inside these ranges and needn't reach their ends.
There are 2 independent parts, one for each index of `groups`. The reference program is written for one: setup_inputs(seed, part) draws one part's arguments, and reference() takes and returns one part's arrays. A program takes and returns all parts, laid end to end along the dimension named above; an argument that names none is the same for every part. Nothing has to cross between parts.
Inputs may be any that keep to these rules, and one draw needn't show every extreme that they name: `sector_table`: sector labels never fall along the rows; each sector covers 1 to 128 consecutive rows.
All inputs are finite; a program needn't handle non-finite values.
Results may differ from the reference program's by a relative error of at most 0.0095.
Values may be sent and summed in bfloat16 or wider, within the bound.
No kernel may reach another device: no remote copies, remote signals or barrier semaphores. Data moves between devices by JAX's collectives and lax.ppermute only.
A program may use at most 64 MiB of HBM per device.

```python
import math
import jax
import jax.numpy as jnp
import numpy as np
from jax import lax

MPO_BOND = 26
LOCAL = 4
PHYS = 16
ROW_DEV = 64
COL_DEV = 128
MPO_DEV = 13
BLOCKS = 4
ROWS = 256
SPAN = 128
SECTORS = 4
COLS = 256
BAND = 192
N_BCOL = 2
N_MPO = 2


def noise_of(key, shape, limit):
    return jnp.clip(jax.random.normal(key, shape, jnp.float32), -limit, limit)


def log_levels(key, count, lower, upper):
    return jnp.exp(jax.random.uniform(key, (count,), jnp.float32, math.log(lower), math.log(upper)))


def draw_amplitudes(key, part):
    key = jax.random.fold_in(key, 11)
    values = noise_of(jax.random.fold_in(key, 1), (ROWS, PHYS, COLS), 6.0)
    block_level = log_levels(jax.random.fold_in(key, 2), ROWS // ROW_DEV, 0.25, 1.4)
    row_level = log_levels(jax.random.fold_in(key, 3), ROWS, 0.7, 1.4)
    slab_level = log_levels(jax.random.fold_in(key, 4), COLS // COL_DEV, 0.6, 1.5)
    row_factor = jnp.repeat(block_level, ROW_DEV) * row_level
    col_factor = jnp.repeat(slab_level, COL_DEV)
    return (values * row_factor[:, None, None] * col_factor[None, None, :]).astype(jnp.bfloat16)


def draw_left_env(key, part):
    key = jax.random.fold_in(key, 12)
    values = noise_of(jax.random.fold_in(key, 1), (MPO_BOND, ROWS, BAND), 3.0) * (2.0 * ROW_DEV) ** (-0.5)
    levels = jax.random.uniform(jax.random.fold_in(key, 2), (ROWS // ROW_DEV,), jnp.float32, -0.2, 1.2)
    row_level = jnp.repeat(levels, ROW_DEV)
    row_pos = jnp.arange(ROWS, dtype=jnp.int32) % ROW_DEV + ROW_DEV
    col_pos = jnp.arange(BAND, dtype=jnp.int32)
    diagonal = (row_pos[:, None] == col_pos[None, :]).astype(jnp.float32) * row_level[:, None]
    return (values + diagonal[None]).astype(jnp.bfloat16)


def draw_right_env(key, part):
    key = jax.random.fold_in(key, 13)
    values = noise_of(jax.random.fold_in(key, 1), (MPO_BOND, COLS, COL_DEV), 2.5) * (1.0 * COL_DEV) ** (-0.5)
    levels = jax.random.uniform(jax.random.fold_in(key, 2), (COLS // COL_DEV,), jnp.float32, 0.4, 1.1)
    row_level = jnp.repeat(levels, COL_DEV)
    row_pos = jnp.arange(COLS, dtype=jnp.int32) % COL_DEV
    col_pos = jnp.arange(COL_DEV, dtype=jnp.int32)
    diagonal = (row_pos[:, None] == col_pos[None, :]).astype(jnp.float32) * row_level[:, None]
    return (values + diagonal[None]).astype(jnp.bfloat16)


def mpo_tensor(key):
    values = noise_of(key, (MPO_BOND, MPO_BOND, LOCAL, LOCAL), 3.0) * 0.3
    bond_eye = jnp.eye(MPO_BOND, dtype=jnp.float32)
    local_eye = jnp.eye(LOCAL, dtype=jnp.float32)
    identity = bond_eye[:, :, None, None] * local_eye[None, None, :, :]
    return (identity + values) * (1.0 * MPO_BOND) ** (-0.5)


def draw_mpo_left(key, part):
    key = jax.random.fold_in(key, 14)
    return mpo_tensor(key)


def draw_mpo_right(key, part):
    key = jax.random.fold_in(key, 15)
    return mpo_tensor(key)


def profile(count, total, bound, lean):
    weights = [(1 << 20) // math.isqrt(standing ** lean) + 1 for standing in range(2, count + 1)]
    rest, given = total - bound - (count - 1), [1] * (count - 1)
    while rest > 0:
        free = [i for i in range(count - 1) if given[i] < bound]
        whole, remaining = sum([weights[i] for i in free]), rest
        for i in free:
            more = min(bound - given[i], max(1, remaining * weights[i] // whole), rest)
            given[i] = given[i] + more
            rest = rest - more
    return np.array([bound] + given)


def ragged(own_key, amount, total, reach, slope):
    if amount == 2:
        one = jax.random.randint(own_key, (), max(1, total - reach), min(reach, total - 1) + 1)
        return jnp.stack([one, total - one])
    lengths = jnp.asarray(profile(amount, total, reach, slope), jnp.int32)
    twos = (amount - 1) // 2
    donor, taker = lengths[1:1 + 2 * twos:2], lengths[2:2 + 2 * twos:2]
    slack = jnp.minimum(donor - 1, reach - taker)
    moved = jax.random.randint(jax.random.fold_in(own_key, 1), (twos,), 0, 1 << 20) % (slack + 1)
    lengths = lengths.at[1:1 + 2 * twos:2].set(donor - moved).at[2:2 + 2 * twos:2].set(taker + moved)
    return lengths[jax.random.permutation(jax.random.fold_in(own_key, 2), amount)]


def setup_inputs(seed: int = 0, part: int = 0) -> dict:
    seeds = jax.random.split(jax.random.key(seed), 7)
    part_keys = jax.random.split(jax.random.fold_in(seeds[6], part), 7)
    amplitudes = draw_amplitudes(jax.random.fold_in(jax.random.fold_in(seeds[6], part), 71), part)
    left_env = draw_left_env(jax.random.fold_in(jax.random.fold_in(seeds[6], part), 71), part)
    right_env = draw_right_env(jax.random.fold_in(jax.random.fold_in(seeds[6], part), 71), part)
    mpo_left = draw_mpo_left(jax.random.fold_in(seeds[6], 71), part)
    mpo_right = draw_mpo_right(jax.random.fold_in(seeds[6], 71), part)
    sector_table = jnp.searchsorted(jnp.cumsum(ragged(part_keys[5], SECTORS, ROWS, SPAN, 0)), jnp.arange(ROWS), side="right").astype(jnp.int32)
    return dict(amplitudes=amplitudes, left_env=left_env, right_env=right_env, mpo_left=mpo_left, mpo_right=mpo_right, sector_table=sector_table)


EPSILON = 1e-06

def coupling_of(mpo_left, mpo_right):
    joined = jnp.einsum('wmik,mvjl->wklvij', mpo_left, mpo_right, precision=lax.Precision.HIGHEST)
    return joined.reshape(MPO_BOND, PHYS, MPO_BOND, PHYS).astype(jnp.bfloat16)

def sector_mask(sector_table):
    outside = jnp.full((ROW_DEV,), -1, dtype=jnp.int32)
    padded = jnp.concatenate([outside, sector_table.astype(jnp.int32), outside])
    lower_labels = padded[:ROWS].reshape(BLOCKS, ROW_DEV)
    own_labels = padded[ROW_DEV:ROWS + ROW_DEV].reshape(BLOCKS, ROW_DEV)
    upper_labels = padded[2 * ROW_DEV:].reshape(BLOCKS, ROW_DEV)
    partner = jnp.concatenate([lower_labels, own_labels, upper_labels], axis=1)
    return own_labels[:, :, None] == partner[:, None, :]

def apply_operator(vector, masked_env, right_env, coupling):
    env_wide = masked_env.astype(jnp.float32)

    def one_slab(slab_index):
        columns = lax.dynamic_slice_in_dim(vector, slab_index * COL_DEV, COL_DEV, 2)
        blocks_view = columns.reshape(BLOCKS, ROW_DEV, PHYS, COL_DEV)
        zero_block = jnp.zeros((1, ROW_DEV, PHYS, COL_DEV), vector.dtype)
        lower_rows = jnp.concatenate([zero_block, blocks_view[:-1]], axis=0)
        upper_rows = jnp.concatenate([blocks_view[1:], zero_block], axis=0)
        extended = jnp.concatenate([lower_rows, blocks_view, upper_rows], axis=1)
        contracted = jnp.einsum('wnak,nksc->wnasc', env_wide, extended.astype(jnp.float32)).astype(jnp.bfloat16)
        slab_env = lax.dynamic_slice_in_dim(right_env, slab_index * COL_DEV, COL_DEV, 1).astype(jnp.float32)
        totals = jnp.zeros((BLOCKS, ROW_DEV, PHYS, COL_DEV), jnp.float32)
        for group_index in range(N_MPO):
            part_t1 = contracted[group_index * MPO_DEV:(group_index + 1) * MPO_DEV].astype(jnp.float32)
            part_c = coupling[group_index * MPO_DEV:(group_index + 1) * MPO_DEV].astype(jnp.float32)

            def add_pair(running, inputs):
                weights_v, env_v = inputs
                mixed_rows = jnp.einsum('wts,wnatc->nasc', weights_v, part_t1).astype(jnp.bfloat16)
                return (running + jnp.einsum('nasc,cd->nasd', mixed_rows.astype(jnp.float32), env_v), None)
            totals, unused = lax.scan(add_pair, totals, (jnp.moveaxis(part_c, 2, 0), slab_env))
        return totals.reshape(ROWS, PHYS, COL_DEV)
    slab_list = lax.map(one_slab, jnp.arange(N_BCOL, dtype=jnp.int32))
    return jnp.transpose(slab_list, (1, 2, 0, 3)).reshape(ROWS, PHYS, COLS)

def reference(amplitudes, left_env, right_env, mpo_left, mpo_right, sector_table):
    entries = ROWS * PHYS * COLS
    coupling = coupling_of(mpo_left, mpo_right)
    band_mask = sector_mask(sector_table)
    shaped_env = left_env.reshape(MPO_BOND, BLOCKS, ROW_DEV, BAND)
    masked_env = jnp.where(band_mask[None], shaped_env, jnp.zeros((), left_env.dtype))
    wide = amplitudes.astype(jnp.float32)
    scale = jnp.sqrt(jnp.sum(wide * wide) / entries + EPSILON)
    basis_one = (wide / scale).astype(jnp.bfloat16)
    image_one = apply_operator(basis_one, masked_env, right_env, coupling)
    first_basis = basis_one.astype(jnp.float32)
    correlation = jnp.sum(first_basis * image_one) / entries
    residual = image_one - correlation * first_basis
    residual_norm = jnp.sqrt(jnp.sum(residual * residual) / entries + EPSILON)
    basis_two = (residual / residual_norm).astype(jnp.bfloat16)
    image_two = apply_operator(basis_two, masked_env, right_env, coupling)
    final_correlation = jnp.sum(basis_two.astype(jnp.float32) * image_two) / entries
    projected = jnp.stack([jnp.stack([correlation, residual_norm]), jnp.stack([residual_norm, final_correlation])])
    return (image_two.astype(jnp.bfloat16), basis_two, projected)
```

```python
import functools

import jax
import jax.numpy as jnp
from jax import lax
from jax.experimental import pallas as pl
from jax.experimental.pallas import tpu as pltpu
from jax.sharding import PartitionSpec as P

EPSILON = 1e-06
SHRINK = 2.0**-12
SLOT = 32
VMEM_LIMIT = 48 * 2**20
ANY = pl.BlockSpec(memory_space=pl.ANY)


def swap_cores(x):
    return lax.ppermute(x, "mpo", [(0, 1), (1, 0)])


def swap_blocks(x):
    blocks = lax.axis_size("brow")
    pairs = []
    for i in range(blocks):
        for core, partner in ((0, i ^ 1), (1, i + 1 if i % 2 else i - 1)):
            if 0 <= partner < blocks:
                pairs.append((2 * i + core, 2 * partner + core))
    return lax.ppermute(x, ("brow", "mpo"), pairs)


def halo_places(rows):
    even = lax.rem(lax.axis_index("brow") + lax.axis_index("mpo"), 2) == 0
    direct = jnp.where(even, 2 * rows, 0)
    return pl.multiple_of(direct, rows), pl.multiple_of(2 * rows - direct, rows)


def apply_steps(env, coupling, right, extended, contracted, mixed, image, waits):
    pairs, depth, width = contracted.shape
    lanes = width // 2
    states = depth // SLOT
    bonds = mixed.shape[1] // lanes

    @pl.loop(0, states // 2)
    def _(step):
        columns = pl.ds(pl.multiple_of(step * width, width), width)
        product = jnp.dot(env[...], extended[:, columns], preferred_element_type=jnp.float32)
        product = product.astype(jnp.bfloat16)
        for row in range(2 * pairs):
            for part in range(2):
                place = pl.ds(pl.multiple_of((2 * step + part) * SLOT, SLOT), SLOT)
                contracted[row // 2, place, row % 2 * lanes : (row % 2 + 1) * lanes] = product[
                    row * SLOT : (row + 1) * SLOT, part * lanes : (part + 1) * lanes
                ]

    waits[0]()

    @pl.loop(0, pairs)
    def _(pair):
        product = jnp.dot(coupling[...], contracted[pair], preferred_element_type=jnp.float32)
        product = product.astype(jnp.bfloat16)
        for part in range(2):
            place = pl.ds(pl.multiple_of((2 * pair + part) * states, states), states)
            for bond in range(bonds):
                mixed[place, bond * lanes : (bond + 1) * lanes] = product[
                    bond * states : (bond + 1) * states, part * lanes : (part + 1) * lanes
                ]

    waits[1]()
    chunk = 128

    @pl.loop(0, image.shape[0] // chunk)
    def _(step):
        place = pl.ds(pl.multiple_of(step * chunk, chunk), chunk)
        image[place, :] = SHRINK * jnp.dot(
            mixed[place, :], right[...], preferred_element_type=jnp.float32
        )


def fetch(pairs, sems):
    copies = [pltpu.make_async_copy(s, d, sems.at[i]) for i, (s, d) in enumerate(pairs)]
    for copy in copies:
        copy.start()
    return copies


def column_sum(x):
    return jnp.sum(x, axis=0, keepdims=True)


def first_kernel(
    env_in, coupling_in, right_in, own_in, direct_in, passed_in,
    image, image_rows, sums,
    env, coupling, right, raw, wide, extended, contracted, mixed, sems,
):
    rows = raw.shape[0] // 3
    states = rows // (extended.shape[0] // 3)
    bond_rows = rows // states
    half = image.shape[0]
    direct, passed = halo_places(bond_rows)
    copies = fetch(
        [
            (own_in, raw.at[pl.ds(rows, rows), :]),
            (direct_in, raw.at[pl.ds(pl.multiple_of(direct * states, rows), rows), :]),
            (passed_in, raw.at[pl.ds(pl.multiple_of(passed * states, rows), rows), :]),
            (env_in, env),
            (coupling_in, coupling),
            (right_in, right),
        ],
        sems,
    )
    for copy in copies[:3]:
        copy.wait()
    lanes = raw.shape[1]
    wide[...] = raw[...].astype(jnp.float32)
    for state in range(states):
        extended[:, state * lanes : (state + 1) * lanes] = wide[
            pl.ds(state, 3 * bond_rows, stride=states), :
        ].astype(jnp.bfloat16)
    copies[3].wait()
    apply_steps(
        env, coupling, right, extended, contracted, mixed, image, (copies[4].wait, copies[5].wait)
    )
    for state in range(states):
        image_rows[:, state * lanes : (state + 1) * lanes] = image[
            pl.ds(state, half // states, stride=states), :
        ].astype(jnp.bfloat16)
    start = pl.multiple_of(rows + lax.axis_index("mpo") * half, half)
    own = wide[pl.ds(start, half), :]
    out = image[...]
    sums[...] = jnp.concatenate(
        [column_sum(own * own), column_sum(own * out), column_sum(out * out)]
        + [jnp.zeros((5, lanes), jnp.float32)],
        axis=0,
    )


def second_kernel(
    env_in, coupling_in, right_in, mine_in, other_in, direct_in, passed_in, first_in, vector_in, sums_in,
    image, sums,
    env, coupling, right, extended, first, vector, contracted, mixed, sems,
):
    bond_rows = extended.shape[0] // 3
    part = bond_rows // 2
    core = lax.axis_index("mpo")
    direct, passed = halo_places(bond_rows)
    mine = pl.multiple_of(bond_rows + core * part, part)
    other = pl.multiple_of(bond_rows + (1 - core) * part, part)
    copies = fetch(
        [
            (mine_in, extended.at[pl.ds(mine, part), :]),
            (other_in, extended.at[pl.ds(other, part), :]),
            (direct_in, extended.at[pl.ds(direct, bond_rows), :]),
            (passed_in, extended.at[pl.ds(passed, bond_rows), :]),
            (env_in, env),
            (coupling_in, coupling),
            (right_in, right),
            (first_in, first),
            (vector_in.at[pl.ds(pl.multiple_of(core * vector.shape[0], vector.shape[0]), vector.shape[0]), :], vector),
        ],
        sems,
    )
    for copy in copies[:5]:
        copy.wait()
    apply_steps(
        env, coupling, right, extended, contracted, mixed, image, (copies[5].wait, copies[6].wait)
    )
    for copy in copies[7:]:
        copy.wait()
    out = image[...]
    lanes = out.shape[1]
    sums[...] = sums_in[...] + jnp.concatenate(
        [jnp.zeros((3, lanes), jnp.float32)]
        + [column_sum(vector[...].astype(jnp.float32) * out), column_sum(first[...] * out)]
        + [jnp.zeros((3, lanes), jnp.float32)],
        axis=0,
    )


def per_device(amplitudes, left_env, right_env, mpo_left, mpo_right, sector_table):
    rows, states, columns = amplitudes.shape
    share, _, band = left_env.shape
    bonds = mpo_left.shape[0]
    half = rows // 2
    half_states = states // 2
    block = lax.axis_index("brow")
    core = lax.axis_index("mpo")
    entries = float(rows * lax.axis_size("brow") * states * columns * lax.axis_size("bcol"))
    flat = amplitudes.reshape(rows * states, columns)

    direct_one = swap_blocks(flat)
    env_there = swap_cores(lax.dynamic_slice_in_dim(left_env, (1 - core) * half, half, 1))
    passed_one = swap_cores(direct_one)

    outside = jnp.full((rows,), -1, dtype=jnp.int32)
    padded = jnp.concatenate([outside, sector_table, outside])
    own_labels = lax.dynamic_slice_in_dim(padded, (block + 1) * rows + core * half, half, 0)
    partner = lax.dynamic_slice_in_dim(padded, block * rows, 3 * rows, 0)
    band_mask = own_labels[:, None] == partner[None, :]
    env_here = lax.dynamic_slice_in_dim(left_env, core * half, half, 1)
    spare = ((0, 0), (0, SLOT // 2 - share), (0, 0))
    env = jnp.concatenate(
        [jnp.pad(jnp.transpose(e, (1, 0, 2)), spare) for e in (env_here, env_there)], axis=1
    )
    env = jnp.where(band_mask[:, None, :], env, jnp.zeros((), env.dtype))
    env = env.reshape(half * SLOT, band)

    def share_of(index):
        piece = lax.dynamic_slice_in_dim(mpo_left, index * share, share, 0)
        return jnp.pad(piece, ((0, SLOT // 2 - share), (0, 0), (0, 0), (0, 0)))

    ordered = jnp.concatenate([share_of(core), share_of(1 - core)], axis=0)
    coupling = jnp.einsum("wmik,mvjl->vijklw", ordered, mpo_right, precision=lax.Precision.HIGHEST)
    coupling = coupling.reshape(bonds * states, states * SLOT).astype(jnp.bfloat16)
    right = right_env.reshape(bonds * columns, columns)

    scratch = [
        pltpu.VMEM((half // 2, states * SLOT, 2 * columns), jnp.bfloat16),
        pltpu.VMEM((half * states, bonds * columns), jnp.bfloat16),
    ]
    held = [
        pltpu.VMEM(env.shape, jnp.bfloat16),
        pltpu.VMEM(coupling.shape, jnp.bfloat16),
        pltpu.VMEM(right.shape, jnp.bfloat16),
    ]
    extended = pltpu.VMEM((3 * rows, states * columns), jnp.bfloat16)
    image_shape = jax.ShapeDtypeStruct((half * states, columns), jnp.float32)
    sums_shape = jax.ShapeDtypeStruct((8, columns), jnp.float32)
    params = pltpu.CompilerParams(vmem_limit_bytes=VMEM_LIMIT)
    whole = pl.BlockSpec(memory_space=pltpu.VMEM)

    first, first_rows, sums = pl.pallas_call(
        first_kernel,
        out_shape=(
            image_shape,
            jax.ShapeDtypeStruct((half, states * columns), jnp.bfloat16),
            sums_shape,
        ),
        in_specs=[ANY] * 6,
        out_specs=(whole,) * 3,
        scratch_shapes=held
        + [
            pltpu.VMEM((3 * rows * states, columns), jnp.bfloat16),
            pltpu.VMEM((3 * rows * states, columns), jnp.float32),
            extended,
        ]
        + scratch
        + [pltpu.SemaphoreType.DMA((6,))],
        compiler_params=params,
        name="first_image",
    )(env, coupling, right, flat, direct_one, passed_one)

    other_rows = swap_cores(first_rows)
    mine_first = core == 0
    block_rows = jnp.concatenate(
        [jnp.where(mine_first, first_rows, other_rows), jnp.where(mine_first, other_rows, first_rows)],
        axis=0,
    )
    direct_two = swap_blocks(block_rows)
    passed_two = swap_cores(direct_two)

    second, sums = pl.pallas_call(
        second_kernel,
        out_shape=(image_shape, sums_shape),
        in_specs=[ANY] * 9 + [whole],
        out_specs=(whole,) * 2,
        scratch_shapes=held
        + [
            extended,
            pltpu.VMEM(image_shape.shape, jnp.float32),
            pltpu.VMEM(image_shape.shape, jnp.bfloat16),
        ]
        + scratch
        + [pltpu.SemaphoreType.DMA((9,))],
        compiler_params=params,
        name="second_image",
    )(env, coupling, right, first_rows, other_rows, direct_two, passed_two, first, flat, sums)

    sums = sums + swap_cores(sums)
    for axis in ("bcol", "brow"):
        size, step = lax.axis_size(axis), 1
        while step < size:
            sums = sums + lax.ppermute(sums, axis, [(i, i ^ step) for i in range(size)])
            step *= 2

    def whole_half(image):
        pieces = image.reshape(half, states, columns)
        kept = lax.dynamic_slice_in_dim(pieces, core * half_states, half_states, 1)
        sent = lax.dynamic_slice_in_dim(pieces, (1 - core) * half_states, half_states, 1)
        got = swap_cores(sent)
        return jnp.concatenate(
            [jnp.where(mine_first, kept, got), jnp.where(mine_first, got, kept)], axis=0
        )

    first_half = whole_half(first)
    second_half = whole_half(second)
    vector_half = lax.dynamic_slice_in_dim(amplitudes, core * half_states, half_states, 1)

    totals = jnp.sum(sums, axis=1)
    s_aa, s_ay, s_yy, s_az, s_yz = (totals[i] for i in range(5))
    scale_sq = s_aa / entries + EPSILON
    shrunk = s_ay / entries / scale_sq
    residual_sq = jnp.maximum(s_yy - 2.0 * shrunk * s_ay + shrunk * shrunk * s_aa, 0.0)
    grow = 1.0 / SHRINK
    residual_norm = jnp.sqrt(residual_sq / scale_sq / entries * (grow * grow) + EPSILON)
    correlation = shrunk * grow
    factor = grow / (jnp.sqrt(scale_sq) * residual_norm)
    basis_two = (first_half - shrunk * vector_half.astype(jnp.float32)) * factor
    image_two = (second_half - shrunk * first_half) * (factor * grow)
    final = (s_yz - shrunk * s_yy - shrunk * s_az + shrunk * shrunk * s_ay) / entries
    final_correlation = final * factor * factor * grow
    projected = jnp.stack(
        [jnp.stack([correlation, residual_norm]), jnp.stack([residual_norm, final_correlation])]
    )
    return (image_two.astype(jnp.bfloat16), basis_two.astype(jnp.bfloat16), projected)


def solution(mesh):
    return jax.shard_map(
        per_device,
        mesh=mesh,
        in_specs=(
            P(("groups", "brow"), None, "bcol"),
            P(("groups", "mpo"), "brow", None),
            P("groups", "bcol", None),
            P(),
            P(),
            P("groups"),
        ),
        out_specs=(
            P(("groups", "brow"), "mpo", "bcol"),
            P(("groups", "brow"), "mpo", "bcol"),
            P("groups", None),
        ),
        check_vma=False,
    )
```

```python
import jax
import jax.numpy as jnp
from jax import lax
from jax.experimental import pallas as pl
from jax.experimental.pallas import tpu as pltpu
from jax.sharding import PartitionSpec as P

EPSILON = 1e-06
SHRINK = 2.0**-12
GROW = 1.0 / SHRINK
SLOT = 32
LOCAL = 4
GROUP = 16
VMEM_LIMIT = 40 * 2**20
WHOLE = pl.BlockSpec(memory_space=pltpu.VMEM)


def swap_cores(x):
    return lax.ppermute(x, "mpo", [(0, 1), (1, 0)])


def swap_blocks(x):
    blocks = lax.axis_size("brow")
    pairs = []
    for i in range(blocks):
        for core, partner in ((0, i ^ 1), (1, i + 1 if i % 2 else i - 1)):
            if 0 <= partner < blocks:
                pairs.append((2 * i + core, 2 * partner + core))
    return lax.ppermute(x, ("brow", "mpo"), pairs)


def halo_places(rows):
    even = lax.rem(lax.axis_index("brow") + lax.axis_index("mpo"), 2) == 0
    direct = jnp.where(even, 2 * rows, 0)
    return pl.multiple_of(direct, rows), pl.multiple_of(2 * rows - direct, rows)


def states_apart(wide, rows, states, store):
    lanes = wide.shape[1]
    for state in range(states):
        piece = wide[pl.ds(state, rows, stride=states), :].astype(jnp.bfloat16)
        store(slice(state * lanes, (state + 1) * lanes), piece)


def prepare_kernel(
    env_mine, env_there, mask, left_mpo, right_mpo, vector,
    env, coupling, vector_rows,
    by_bond, wide, left_pad, right_pad, left_rows, right_rows, spread,
):
    core = lax.axis_index("mpo")
    share, rows, _ = env_mine.shape
    half = rows // 2
    here = pl.ds(pl.multiple_of(core * half, half), half)
    part = SLOT // 2
    band = mask.shape[1]
    by_bond[...] = jnp.zeros_like(by_bond)
    for low in range(0, band, 128):
        width = min(128, band - low)
        base = low // 128 * SLOT * half
        for group, source in enumerate((env_mine, env_there)):
            for bond in range(share):
                start = base + (group * part + bond) * half
                piece = source[bond, here, low : low + width].astype(jnp.float32)
                by_bond[start : start + half, 0:width] = piece
        for row in range(half):
            piece = by_bond[pl.ds(base + row, SLOT, stride=half), :][:, 0:width]
            kept = jnp.where(mask[row : row + 1, low : low + width] > 0.0, piece, 0.0)
            env[row * SLOT : (row + 1) * SLOT, low : low + width] = kept.astype(jnp.bfloat16)

    states = vector.shape[0] // rows
    wide[...] = vector[...].astype(jnp.float32)

    def store(columns, piece):
        vector_rows[:, columns] = piece

    states_apart(wide, rows, states, store)

    used, bonds = left_mpo.shape
    left_pad[...] = jnp.zeros_like(left_pad)
    right_pad[...] = jnp.zeros_like(right_pad)
    left_pad[0:used, 0:bonds] = left_mpo[...]
    right_pad[0:used, 0:bonds] = right_mpo[...]
    for state in range(states):
        for group, owner in enumerate((core, 1 - core)):
            start = state * SLOT + group * part
            left_rows[start : start + part, :] = left_pad[
                pl.ds(owner * (share * states) + state, part, stride=states), :
            ]
        across = right_pad[pl.ds(state, SLOT, stride=states), :]
        right_rows[state * SLOT : (state + 1) * SLOT, :] = jnp.transpose(across)[0:SLOT, :]
    joined = lax.dot_general(
        right_rows[...],
        left_rows[:, 0:SLOT],
        (((1,), (1,)), ((), ())),
        precision=lax.Precision.HIGHEST,
        preferred_element_type=jnp.float32,
    )
    width = LOCAL * SLOT
    for i in range(LOCAL):
        for j in range(LOCAL):
            for inner in range(LOCAL):
                start = inner * SLOT * states + i * LOCAL + j
                spread[pl.ds(start, SLOT, stride=states), :] = joined[
                    (j * LOCAL + inner) * SLOT : (j * LOCAL + inner + 1) * SLOT,
                    i * width : (i + 1) * width,
                ]
    for inner in range(LOCAL):
        start = inner * SLOT * states
        coupling[:, inner * width : (inner + 1) * width] = spread[
            start : start + used, :
        ].astype(jnp.bfloat16)


def apply_steps(env, coupling, right, extended, contracted, mixed):
    groups, depth, width = contracted.shape
    lanes = right.shape[1]
    group = width // lanes
    states = depth // SLOT
    bonds = mixed.shape[1] // lanes
    product = jnp.dot(env[...], extended[...], preferred_element_type=jnp.float32)
    product = product.astype(jnp.bfloat16)
    for state in range(states):
        place = state % LOCAL * LOCAL + state // LOCAL
        for row in range(groups * group):
            contracted[
                row // group,
                place * SLOT : (place + 1) * SLOT,
                row % group * lanes : (row % group + 1) * lanes,
            ] = product[row * SLOT : (row + 1) * SLOT, state * lanes : (state + 1) * lanes]

    @pl.loop(0, groups)
    def _(step):
        product = jnp.dot(coupling[...], contracted[step], preferred_element_type=jnp.float32)
        product = product.astype(jnp.bfloat16)
        for part in range(group):
            place = pl.ds(pl.multiple_of((group * step + part) * states, states), states)
            for bond in range(bonds):
                mixed[place, bond * lanes : (bond + 1) * lanes] = product[
                    bond * states : (bond + 1) * states, part * lanes : (part + 1) * lanes
                ]

    return SHRINK * jnp.dot(mixed[...], right[...], preferred_element_type=jnp.float32)


def column_sum(x):
    return jnp.sum(x, axis=0, keepdims=True)


def send_half(image, states):
    lanes = image.shape[1]
    pieces = image.reshape(image.shape[0] // states, states, lanes)
    low, high = pieces[:, : states // 2, :], pieces[:, states // 2 :, :]
    first = lax.axis_index("mpo") == 0
    return jnp.where(first, high, low), jnp.where(first, low, high)


def first_kernel(
    env, coupling, right, vector, vector_rows, direct_in, passed_in,
    image, image_rows, sent, kept, sums,
    wide, extended, contracted, mixed,
):
    rows = vector_rows.shape[0]
    states = vector.shape[0] // rows
    half = image.shape[0]
    extended[rows : 2 * rows, :] = vector_rows[...]
    for place, source in zip(halo_places(rows), (direct_in, passed_in)):
        wide[...] = source[...].astype(jnp.float32)

        def store(columns, piece, place=place):
            extended[pl.ds(place, rows), columns] = piece

        states_apart(wide, rows, states, store)
    out = apply_steps(env, coupling, right, extended, contracted, mixed)
    image[...] = out

    def store_rows(columns, piece):
        image_rows[:, columns] = piece

    states_apart(image, half // states, states, store_rows)
    sent[...], kept[...] = send_half(out, states)
    start = pl.multiple_of(lax.axis_index("mpo") * half, half)
    own = vector[pl.ds(start, half), :].astype(jnp.float32)
    lanes = out.shape[1]
    sums[...] = jnp.concatenate(
        [column_sum(own * own), column_sum(own * out), column_sum(out * out)]
        + [jnp.zeros((5, lanes), jnp.float32)],
        axis=0,
    )


def second_kernel(
    env, coupling, right, mine_in, other_in, direct_in, passed_in, first, vector, sums,
    sent, kept, totals,
    extended, contracted, mixed,
):
    rows = direct_in.shape[0]
    part = rows // 2
    half = first.shape[0]
    core = lax.axis_index("mpo")
    direct, passed = halo_places(rows)
    mine = pl.multiple_of(rows + core * part, part)
    other = pl.multiple_of(rows + (1 - core) * part, part)
    extended[pl.ds(mine, part), :] = mine_in[...]
    extended[pl.ds(other, part), :] = other_in[...]
    extended[pl.ds(direct, rows), :] = direct_in[...]
    extended[pl.ds(passed, rows), :] = passed_in[...]
    out = apply_steps(env, coupling, right, extended, contracted, mixed)
    sent[...], kept[...] = send_half(out, half // part)
    own = vector[pl.ds(pl.multiple_of(core * half, half), half), :].astype(jnp.float32)
    lanes = out.shape[1]
    columns = jnp.concatenate(
        [sums[0:3, :], column_sum(own * out), column_sum(first[...] * out)]
        + [jnp.zeros((3, lanes), jnp.float32)],
        axis=0,
    )
    lane = lax.broadcasted_iota(jnp.int32, columns.shape, 1)
    row = lax.broadcasted_iota(jnp.int32, columns.shape, 0)
    spread = jnp.where(lane == row, jnp.sum(columns, axis=1, keepdims=True), 0.0)
    totals[...] = jnp.broadcast_to(column_sum(spread)[None], totals.shape)


def final_kernel(
    entries, first_kept, first_got, second_kept, second_got, vector, gathered,
    image_two, basis_two, projected,
):
    half, half_states, lanes = first_kept.shape
    core = lax.axis_index("mpo")
    totals = column_sum(jnp.sum(gathered[...], axis=0))
    lane = lax.broadcasted_iota(jnp.int32, totals.shape, 1)

    def total(index):
        return jnp.sum(jnp.where(lane == index, totals, 0.0), axis=1, keepdims=True)

    s_aa, s_ay, s_yy, s_az, s_yz = (total(i) for i in range(5))
    scale_sq = s_aa / entries + EPSILON
    shrunk = s_ay / entries / scale_sq
    residual_sq = jnp.maximum(s_yy - 2.0 * shrunk * s_ay + shrunk * shrunk * s_aa, 0.0)
    residual_norm = jnp.sqrt(residual_sq / scale_sq / entries * (GROW * GROW) + EPSILON)
    factor = GROW / (jnp.sqrt(scale_sq) * residual_norm)
    final = (s_yz - shrunk * s_yy - shrunk * s_az + shrunk * shrunk * s_ay) / entries
    gamma = final * factor * factor * GROW
    r = lax.broadcasted_iota(jnp.int32, projected.shape, 0)
    c = lax.broadcasted_iota(jnp.int32, projected.shape, 1)
    diagonal = jnp.where(r == 0, shrunk * GROW, gamma)
    projected[...] = jnp.where(r == c, diagonal, residual_norm)

    size = half * half_states
    wide = vector[...].astype(jnp.float32).reshape(2 * half, 2 * half_states, lanes)
    own = jnp.where(core == 0, wide[:, :half_states, :], wide[:, half_states:, :])
    own = own.reshape(2 * size, lanes)
    ours = jnp.where(core == 0, own[:size, :], own[size:, :])
    theirs = jnp.where(core == 0, own[size:, :], own[:size, :])
    for index, y_ref, z_ref, a in (
        (core, first_kept, second_kept, ours),
        (1 - core, first_got, second_got, theirs),
    ):
        y = y_ref[...].reshape(size, lanes)
        z = z_ref[...].reshape(size, lanes)
        place = pl.ds(pl.multiple_of(index * size, size), size)
        basis_two[place, :] = ((y - shrunk * a) * factor).astype(jnp.bfloat16)
        image_two[place, :] = ((z - shrunk * y) * (factor * GROW)).astype(jnp.bfloat16)


def call(kernel, operands, outs, scratch, name):
    return pl.pallas_call(
        kernel,
        out_shape=tuple(jax.ShapeDtypeStruct(shape, dtype) for shape, dtype in outs),
        in_specs=[WHOLE] * len(operands),
        out_specs=(WHOLE,) * len(outs),
        scratch_shapes=[pltpu.VMEM(shape, dtype) for shape, dtype in scratch],
        compiler_params=pltpu.CompilerParams(vmem_limit_bytes=VMEM_LIMIT),
        name=name,
    )(*operands)


def per_device(amplitudes, left_env, right_env, mpo_left, mpo_right, sector_table):
    rows, states, columns = amplitudes.shape
    band = left_env.shape[2]
    bonds = mpo_left.shape[0]
    half = rows // 2
    half_states = states // 2
    size = half * states
    block = lax.axis_index("brow")
    core = lax.axis_index("mpo")
    axes = ("brow", "bcol", "mpo")
    peers = lax.axis_size(axes)
    entries = float(rows * lax.axis_size("brow") * states * columns * lax.axis_size("bcol"))
    f32, bf16 = jnp.float32, jnp.bfloat16
    flat = amplitudes.reshape(rows * states, columns)

    env_there = swap_cores(left_env)
    direct_one = swap_blocks(flat)
    passed_one = swap_cores(direct_one)

    outside = jnp.full((rows,), -1, dtype=jnp.int32)
    padded = jnp.concatenate([outside, sector_table, outside])
    own_labels = lax.dynamic_slice_in_dim(padded, (block + 1) * rows + core * half, half, 0)
    partner = lax.dynamic_slice_in_dim(padded, block * rows, 3 * rows, 0)
    mask = (own_labels[:, None] == partner[None, :]).astype(f32)
    left_rows = jnp.transpose(mpo_left, (0, 2, 3, 1)).reshape(bonds * states, bonds)
    right_rows = jnp.transpose(mpo_right, (0, 2, 3, 1)).reshape(bonds * states, bonds)
    env, coupling, vector_rows = call(
        prepare_kernel,
        (left_env, env_there, mask, left_rows, right_rows, flat),
        (
            ((half * SLOT, band), bf16),
            ((bonds * states, states * SLOT), bf16),
            ((rows, states * columns), bf16),
        ),
        (
            ((-(-band // 128) * SLOT * half, 128), f32),
            ((rows * states, columns), f32),
            ((SLOT * states, 128), f32),
            ((SLOT * states, 128), f32),
            ((states * SLOT, 128), f32),
            ((states * SLOT, SLOT), f32),
            ((states // LOCAL * SLOT * states, 128), f32),
        ),
        "operands",
    )
    right = right_env.reshape(bonds * columns, columns)

    work = (
        ((3 * rows, states * columns), bf16),
        ((half // GROUP, states * SLOT, GROUP * columns), bf16),
        ((size, bonds * columns), bf16),
    )
    half_shape = ((half, half_states, columns), f32)
    first, first_rows, first_sent, first_kept, sums = call(
        first_kernel,
        (env, coupling, right, flat, vector_rows, direct_one, passed_one),
        (
            ((size, columns), f32),
            ((half, states * columns), bf16),
            half_shape,
            half_shape,
            ((8, columns), f32),
        ),
        (((rows * states, columns), f32),) + work,
        "first_image",
    )

    other_rows = swap_cores(first_rows)
    mine_first = core == 0
    block_rows = jnp.concatenate(
        [jnp.where(mine_first, first_rows, other_rows), jnp.where(mine_first, other_rows, first_rows)],
        axis=0,
    )
    direct_two = swap_blocks(block_rows)
    first_got = swap_cores(first_sent)
    passed_two = swap_cores(direct_two)

    second_sent, second_kept, totals = call(
        second_kernel,
        (env, coupling, right, first_rows, other_rows, direct_two, passed_two, first, flat, sums),
        (half_shape, half_shape, ((peers, 1, columns), f32)),
        work,
        "second_image",
    )
    second_got = swap_cores(second_sent)
    gathered = lax.all_to_all(totals, axes, 0, 0)

    def finish(*refs):
        final_kernel(entries, *refs)

    image_two, basis_two, projected = call(
        finish,
        (first_kept, first_got, second_kept, second_got, flat, gathered),
        (
            ((rows * half_states, columns), bf16),
            ((rows * half_states, columns), bf16),
            ((2, 2), f32),
        ),
        (),
        "outputs",
    )
    shape = (rows, half_states, columns)
    return (image_two.reshape(shape), basis_two.reshape(shape), projected)


def solution(mesh):
    return jax.shard_map(
        per_device,
        mesh=mesh,
        in_specs=(
            P(("groups", "brow"), None, "bcol"),
            P(("groups", "mpo"), "brow", None),
            P("groups", "bcol", None),
            P(),
            P(),
            P("groups"),
        ),
        out_specs=(
            P(("groups", "brow"), "mpo", "bcol"),
            P(("groups", "brow"), "mpo", "bcol"),
            P("groups", None),
        ),
        check_vma=False,
    )
```

```python
import jax
import jax.numpy as jnp
from jax import lax
from jax.experimental import pallas as pl
from jax.experimental.pallas import tpu as pltpu
from jax.sharding import PartitionSpec as P

EPSILON = 1e-06
SHRINK = 2.0**-12
GROW = 1.0 / SHRINK
SLOT = 32
LOCAL = 4
GROUP = 16
VMEM_LIMIT = 40 * 2**20
WHOLE = pl.BlockSpec(memory_space=pltpu.VMEM)


def swap_cores(x):
    return lax.ppermute(x, "mpo", [(0, 1), (1, 0)])


def swap_blocks(x):
    blocks = lax.axis_size("brow")
    pairs = []
    for i in range(blocks):
        for core, partner in ((0, i ^ 1), (1, i + 1 if i % 2 else i - 1)):
            if 0 <= partner < blocks:
                pairs.append((2 * i + core, 2 * partner + core))
    return lax.ppermute(x, ("brow", "mpo"), pairs)


def halo_places(rows):
    even = lax.rem(lax.axis_index("brow") + lax.axis_index("mpo"), 2) == 0
    direct = jnp.where(even, 2 * rows, 0)
    return pl.multiple_of(direct, rows), pl.multiple_of(2 * rows - direct, rows)


def states_apart(wide, rows, states, store):
    lanes = wide.shape[1]
    for state in range(states):
        piece = wide[pl.ds(state, rows, stride=states), :].astype(jnp.bfloat16)
        store(slice(state * lanes, (state + 1) * lanes), piece)


def prepare_kernel(
    env_mine, env_there, mask, both_mpo,
    env, coupling,
    by_bond, left_pad, right_pad, left_rows, right_rows, spread,
):
    core = lax.axis_index("mpo")
    share, rows, _ = env_mine.shape
    half = rows // 2
    here = pl.ds(pl.multiple_of(core * half, half), half)
    part = SLOT // 2
    used, bonds = both_mpo.shape[0] // 2, both_mpo.shape[1]
    states = used // bonds
    left_pad[...] = jnp.zeros_like(left_pad)
    right_pad[...] = jnp.zeros_like(right_pad)
    left_pad[0:used, 0:bonds] = both_mpo[0:used, :]
    right_pad[0:used, 0:bonds] = both_mpo[used : 2 * used, :]
    for state in range(states):
        for group, owner in enumerate((core, 1 - core)):
            start = state * SLOT + group * part
            left_rows[start : start + part, :] = left_pad[
                pl.ds(owner * (share * states) + state, part, stride=states), :
            ]
        across = right_pad[pl.ds(state, SLOT, stride=states), :]
        right_rows[state * SLOT : (state + 1) * SLOT, :] = jnp.transpose(across)[0:SLOT, :]
    joined = lax.dot_general(
        right_rows[...],
        left_rows[:, 0:SLOT],
        (((1,), (1,)), ((), ())),
        precision=lax.Precision.HIGHEST,
        preferred_element_type=jnp.float32,
    )
    width = LOCAL * SLOT
    for i in range(LOCAL):
        for j in range(LOCAL):
            for inner in range(LOCAL):
                start = inner * SLOT * states + i * LOCAL + j
                spread[pl.ds(start, SLOT, stride=states), :] = joined[
                    (j * LOCAL + inner) * SLOT : (j * LOCAL + inner + 1) * SLOT,
                    i * width : (i + 1) * width,
                ]
    for inner in range(LOCAL):
        start = inner * SLOT * states
        coupling[:, inner * width : (inner + 1) * width] = spread[
            start : start + used, :
        ].astype(jnp.bfloat16)

    band = mask.shape[1]
    by_bond[...] = jnp.zeros_like(by_bond)
    for low in range(0, band, 128):
        width = min(128, band - low)
        base = low // 128 * SLOT * half
        for group, source in enumerate((env_mine, env_there)):
            for bond in range(share):
                start = base + (group * part + bond) * half
                piece = source[bond, here, low : low + width].astype(jnp.float32)
                by_bond[start : start + half, 0:width] = piece
        for row in range(half):
            piece = by_bond[pl.ds(base + row, SLOT, stride=half), :][:, 0:width]
            kept = jnp.where(mask[row : row + 1, low : low + width] > 0.0, piece, 0.0)
            env[row * SLOT : (row + 1) * SLOT, low : low + width] = kept.astype(jnp.bfloat16)


def apply_steps(env, coupling, right, extended, contracted, mixed):
    groups, depth, width = contracted.shape
    lanes = right.shape[1]
    group = width // lanes
    states = depth // SLOT
    bonds = mixed.shape[1] // lanes
    product = jnp.dot(env[...], extended[...], preferred_element_type=jnp.float32)
    product = product.astype(jnp.bfloat16)
    for state in range(states):
        place = state % LOCAL * LOCAL + state // LOCAL
        for row in range(groups * group):
            contracted[
                row // group,
                place * SLOT : (place + 1) * SLOT,
                row % group * lanes : (row % group + 1) * lanes,
            ] = product[row * SLOT : (row + 1) * SLOT, state * lanes : (state + 1) * lanes]

    @pl.loop(0, groups)
    def _(step):
        product = jnp.dot(coupling[...], contracted[step], preferred_element_type=jnp.float32)
        product = product.astype(jnp.bfloat16)
        for part in range(group):
            place = pl.ds(pl.multiple_of((group * step + part) * states, states), states)
            for bond in range(bonds):
                mixed[place, bond * lanes : (bond + 1) * lanes] = product[
                    bond * states : (bond + 1) * states, part * lanes : (part + 1) * lanes
                ]

    return SHRINK * jnp.dot(mixed[...], right[...], preferred_element_type=jnp.float32)


def column_sum(x):
    return jnp.sum(x, axis=0, keepdims=True)


def send_half(image, states):
    lanes = image.shape[1]
    pieces = image.reshape(image.shape[0] // states, states, lanes)
    low, high = pieces[:, : states // 2, :], pieces[:, states // 2 :, :]
    first = lax.axis_index("mpo") == 0
    return jnp.where(first, high, low), jnp.where(first, low, high)


def first_kernel(
    env, coupling, right, vector, direct_in, passed_in,
    image, image_rows, sent, kept, sums,
    wide, extended, contracted, mixed,
):
    rows = extended.shape[0] // 3
    states = vector.shape[0] // rows
    half = image.shape[0]
    for place, source in zip((rows,) + halo_places(rows), (vector, direct_in, passed_in)):
        wide[...] = source[...].astype(jnp.float32)

        def store(columns, piece, place=place):
            extended[pl.ds(place, rows), columns] = piece

        states_apart(wide, rows, states, store)
    out = apply_steps(env, coupling, right, extended, contracted, mixed)
    image[...] = out

    def store_rows(columns, piece):
        image_rows[:, columns] = piece

    states_apart(image, half // states, states, store_rows)
    sent[...], kept[...] = send_half(out, states)
    start = pl.multiple_of(lax.axis_index("mpo") * half, half)
    own = vector[pl.ds(start, half), :].astype(jnp.float32)
    lanes = out.shape[1]
    sums[...] = jnp.concatenate(
        [column_sum(own * own), column_sum(own * out), column_sum(out * out)]
        + [jnp.zeros((5, lanes), jnp.float32)],
        axis=0,
    )


def second_kernel(
    env, coupling, right, mine_in, other_in, direct_in, passed_in, first, vector, sums,
    sent, kept, totals,
    extended, contracted, mixed,
):
    rows = direct_in.shape[0]
    part = rows // 2
    half = first.shape[0]
    core = lax.axis_index("mpo")
    direct, passed = halo_places(rows)
    mine = pl.multiple_of(rows + core * part, part)
    other = pl.multiple_of(rows + (1 - core) * part, part)
    extended[pl.ds(mine, part), :] = mine_in[...]
    extended[pl.ds(other, part), :] = other_in[...]
    extended[pl.ds(direct, rows), :] = direct_in[...]
    extended[pl.ds(passed, rows), :] = passed_in[...]
    out = apply_steps(env, coupling, right, extended, contracted, mixed)
    sent[...], kept[...] = send_half(out, half // part)
    own = vector[pl.ds(pl.multiple_of(core * half, half), half), :].astype(jnp.float32)
    lanes = out.shape[1]
    columns = jnp.concatenate(
        [sums[0:3, :], column_sum(own * out), column_sum(first[...] * out)]
        + [jnp.zeros((3, lanes), jnp.float32)],
        axis=0,
    )
    lane = lax.broadcasted_iota(jnp.int32, columns.shape, 1)
    row = lax.broadcasted_iota(jnp.int32, columns.shape, 0)
    spread = jnp.where(lane == row, jnp.sum(columns, axis=1, keepdims=True), 0.0)
    totals[...] = jnp.broadcast_to(column_sum(spread)[None], totals.shape)


def final_kernel(
    entries, first_kept, first_got, second_kept, second_got, vector, gathered,
    image_two, basis_two, projected,
):
    half, half_states, lanes = first_kept.shape
    core = lax.axis_index("mpo")
    totals = column_sum(jnp.sum(gathered[...], axis=0))
    lane = lax.broadcasted_iota(jnp.int32, totals.shape, 1)

    def total(index):
        return jnp.sum(jnp.where(lane == index, totals, 0.0), axis=1, keepdims=True)

    s_aa, s_ay, s_yy, s_az, s_yz = (total(i) for i in range(5))
    scale_sq = s_aa / entries + EPSILON
    shrunk = s_ay / entries / scale_sq
    residual_sq = jnp.maximum(s_yy - 2.0 * shrunk * s_ay + shrunk * shrunk * s_aa, 0.0)
    residual_norm = jnp.sqrt(residual_sq / scale_sq / entries * (GROW * GROW) + EPSILON)
    factor = GROW / (jnp.sqrt(scale_sq) * residual_norm)
    final = (s_yz - shrunk * s_yy - shrunk * s_az + shrunk * shrunk * s_ay) / entries
    gamma = final * factor * factor * GROW
    r = lax.broadcasted_iota(jnp.int32, projected.shape, 0)
    c = lax.broadcasted_iota(jnp.int32, projected.shape, 1)
    diagonal = jnp.where(r == 0, shrunk * GROW, gamma)
    projected[...] = jnp.where(r == c, diagonal, residual_norm)

    size = half * half_states
    wide = vector[...].astype(jnp.float32).reshape(2 * half, 2 * half_states, lanes)
    own = jnp.where(core == 0, wide[:, :half_states, :], wide[:, half_states:, :])
    own = own.reshape(2 * size, lanes)
    ours = jnp.where(core == 0, own[:size, :], own[size:, :])
    theirs = jnp.where(core == 0, own[size:, :], own[:size, :])
    for index, y_ref, z_ref, a in (
        (core, first_kept, second_kept, ours),
        (1 - core, first_got, second_got, theirs),
    ):
        y = y_ref[...].reshape(size, lanes)
        z = z_ref[...].reshape(size, lanes)
        place = pl.ds(pl.multiple_of(index * size, size), size)
        basis_two[place, :] = ((y - shrunk * a) * factor).astype(jnp.bfloat16)
        image_two[place, :] = ((z - shrunk * y) * (factor * GROW)).astype(jnp.bfloat16)


def call(kernel, operands, outs, scratch, name, cost=None):
    return pl.pallas_call(
        kernel,
        out_shape=tuple(jax.ShapeDtypeStruct(shape, dtype) for shape, dtype in outs),
        in_specs=[WHOLE] * len(operands),
        out_specs=(WHOLE,) * len(outs),
        scratch_shapes=[pltpu.VMEM(shape, dtype) for shape, dtype in scratch],
        cost_estimate=cost,
        compiler_params=pltpu.CompilerParams(vmem_limit_bytes=VMEM_LIMIT),
        name=name,
    )(*operands)


def per_device(amplitudes, left_env, right_env, mpo_left, mpo_right, sector_table):
    rows, states, columns = amplitudes.shape
    band = left_env.shape[2]
    bonds = mpo_left.shape[0]
    half = rows // 2
    half_states = states // 2
    size = half * states
    block = lax.axis_index("brow")
    core = lax.axis_index("mpo")
    axes = ("brow", "bcol", "mpo")
    peers = lax.axis_size(axes)
    entries = float(rows * lax.axis_size("brow") * states * columns * lax.axis_size("bcol"))
    f32, bf16 = jnp.float32, jnp.bfloat16
    flat = amplitudes.reshape(rows * states, columns)

    env_there = swap_cores(left_env)
    direct_one = swap_blocks(flat)

    outside = jnp.full((rows,), -1, dtype=jnp.int32)
    padded = jnp.concatenate([outside, sector_table, outside])
    own_labels = lax.dynamic_slice_in_dim(padded, (block + 1) * rows + core * half, half, 0)
    partner = lax.dynamic_slice_in_dim(padded, block * rows, 3 * rows, 0)
    mask = (own_labels[:, None] == partner[None, :]).astype(f32)
    both = jnp.concatenate([mpo_left, mpo_right], axis=0)
    both = jnp.transpose(both, (0, 2, 3, 1)).reshape(2 * bonds * states, bonds)
    env, coupling = call(
        prepare_kernel,
        (left_env, env_there, mask, both),
        (
            ((half * SLOT, band), bf16),
            ((bonds * states, states * SLOT), bf16),
        ),
        (
            ((-(-band // 128) * SLOT * half, 128), f32),
            ((SLOT * states, 128), f32),
            ((SLOT * states, 128), f32),
            ((states * SLOT, 128), f32),
            ((states * SLOT, SLOT), f32),
            ((states // LOCAL * SLOT * states, 128), f32),
        ),
        "operands",
        cost=pl.CostEstimate(flops=4 * 10**9, bytes_accessed=2**23, transcendentals=0),
    )
    direct_one, env, coupling = lax.optimization_barrier((direct_one, env, coupling))
    passed_one = swap_cores(direct_one)
    right = right_env.reshape(bonds * columns, columns)

    work = (
        ((3 * rows, states * columns), bf16),
        ((half // GROUP, states * SLOT, GROUP * columns), bf16),
        ((size, bonds * columns), bf16),
    )
    half_shape = ((half, half_states, columns), f32)
    first, first_rows, first_sent, first_kept, sums = call(
        first_kernel,
        (env, coupling, right, flat, direct_one, passed_one),
        (
            ((size, columns), f32),
            ((half, states * columns), bf16),
            half_shape,
            half_shape,
            ((8, columns), f32),
        ),
        (((rows * states, columns), f32),) + work,
        "first_image",
    )

    other_rows = swap_cores(first_rows)
    mine_first = core == 0
    block_rows = jnp.concatenate(
        [jnp.where(mine_first, first_rows, other_rows), jnp.where(mine_first, other_rows, first_rows)],
        axis=0,
    )
    direct_two = swap_blocks(block_rows)
    first_got = swap_cores(first_sent)
    passed_two = swap_cores(direct_two)

    second_sent, second_kept, totals = call(
        second_kernel,
        (env, coupling, right, first_rows, other_rows, direct_two, passed_two, first, flat, sums),
        (half_shape, half_shape, ((peers, 1, columns), f32)),
        work,
        "second_image",
    )
    second_got = swap_cores(second_sent)
    gathered = lax.all_to_all(totals, axes, 0, 0)

    def finish(*refs):
        final_kernel(entries, *refs)

    image_two, basis_two, projected = call(
        finish,
        (first_kept, first_got, second_kept, second_got, flat, gathered),
        (
            ((rows * half_states, columns), bf16),
            ((rows * half_states, columns), bf16),
            ((2, 2), f32),
        ),
        (),
        "outputs",
    )
    shape = (rows, half_states, columns)
    return (image_two.reshape(shape), basis_two.reshape(shape), projected)


def solution(mesh):
    return jax.shard_map(
        per_device,
        mesh=mesh,
        in_specs=(
            P(("groups", "brow"), None, "bcol"),
            P(("groups", "mpo"), "brow", None),
            P("groups", "bcol", None),
            P(),
            P(),
            P("groups"),
        ),
        out_specs=(
            P(("groups", "brow"), "mpo", "bcol"),
            P(("groups", "brow"), "mpo", "bcol"),
            P("groups", None),
        ),
        check_vma=False,
    )
```

```python
import jax
import jax.numpy as jnp
from jax import lax
from jax.experimental import pallas as pl
from jax.experimental.pallas import tpu as pltpu
from jax.sharding import PartitionSpec as P

EPSILON = 1e-06
SHRINK = 2.0**-12
GROW = 1.0 / SHRINK
SLOT = 32
LOCAL = 4
GROUP = 8
VMEM_LIMIT = 40 * 2**20
WHOLE = pl.BlockSpec(memory_space=pltpu.VMEM)


def swap_cores(x):
    return lax.ppermute(x, "mpo", [(0, 1), (1, 0)])


def swap_blocks(x):
    blocks = lax.axis_size("brow")
    pairs = []
    for i in range(blocks):
        for core, partner in ((0, i ^ 1), (1, i + 1 if i % 2 else i - 1)):
            if 0 <= partner < blocks:
                pairs.append((2 * i + core, 2 * partner + core))
    return lax.ppermute(x, ("brow", "mpo"), pairs)


def halo_places(rows):
    even = lax.rem(lax.axis_index("brow") + lax.axis_index("mpo"), 2) == 0
    direct = jnp.where(even, 2 * rows, 0)
    return pl.multiple_of(direct, rows), pl.multiple_of(2 * rows - direct, rows)


def states_apart(wide, rows, states, store):
    lanes = wide.shape[1]
    for state in range(states):
        piece = wide[pl.ds(state, rows, stride=states), :].astype(jnp.bfloat16)
        store(slice(state * lanes, (state + 1) * lanes), piece)


def prepare_kernel(
    env_mine, env_there, mask, both_mpo,
    env, coupling,
    by_bond, left_pad, right_pad, left_rows, right_rows, spread,
):
    core = lax.axis_index("mpo")
    share, rows, _ = env_mine.shape
    half = rows // 2
    here = pl.ds(pl.multiple_of(core * half, half), half)
    part = SLOT // 2
    used, bonds = both_mpo.shape[0] // 2, both_mpo.shape[1]
    states = used // bonds
    left_pad[...] = jnp.zeros_like(left_pad)
    right_pad[...] = jnp.zeros_like(right_pad)
    left_pad[0:used, 0:bonds] = both_mpo[0:used, :]
    right_pad[0:used, 0:bonds] = both_mpo[used : 2 * used, :]
    for state in range(states):
        for group, owner in enumerate((core, 1 - core)):
            start = state * SLOT + group * part
            left_rows[start : start + part, :] = left_pad[
                pl.ds(owner * (share * states) + state, part, stride=states), :
            ]
        across = right_pad[pl.ds(state, SLOT, stride=states), :]
        right_rows[state * SLOT : (state + 1) * SLOT, :] = jnp.transpose(across)[0:SLOT, :]
    joined = lax.dot_general(
        right_rows[...],
        left_rows[:, 0:SLOT],
        (((1,), (1,)), ((), ())),
        precision=lax.Precision.HIGHEST,
        preferred_element_type=jnp.float32,
    )
    width = LOCAL * SLOT
    for i in range(LOCAL):
        for j in range(LOCAL):
            for inner in range(LOCAL):
                start = inner * SLOT * states + i * LOCAL + j
                spread[pl.ds(start, SLOT, stride=states), :] = joined[
                    (j * LOCAL + inner) * SLOT : (j * LOCAL + inner + 1) * SLOT,
                    i * width : (i + 1) * width,
                ]
    for inner in range(LOCAL):
        start = inner * SLOT * states
        coupling[:, inner * width : (inner + 1) * width] = spread[
            start : start + used, :
        ].astype(jnp.bfloat16)

    band = mask.shape[1]
    by_bond[...] = jnp.zeros_like(by_bond)
    for low in range(0, band, 128):
        width = min(128, band - low)
        base = low // 128 * SLOT * half
        for group, source in enumerate((env_mine, env_there)):
            for bond in range(share):
                start = base + (group * part + bond) * half
                piece = source[bond, here, low : low + width].astype(jnp.float32)
                by_bond[start : start + half, 0:width] = piece
        for row in range(half):
            piece = by_bond[pl.ds(base + row, SLOT, stride=half), :][:, 0:width]
            kept = jnp.where(mask[row : row + 1, low : low + width] > 0.0, piece, 0.0)
            env[row * SLOT : (row + 1) * SLOT, low : low + width] = kept.astype(jnp.bfloat16)


def apply_steps(env, coupling, right, extended, contracted, mixed, image):
    groups, depth, width = contracted.shape
    lanes = right.shape[1]
    group = width // lanes
    states = depth // SLOT
    bonds = mixed.shape[1] // lanes
    product = jnp.dot(env[...], extended[...], preferred_element_type=jnp.float32)
    product = product.astype(jnp.bfloat16)
    for state in range(states):
        place = state % LOCAL * LOCAL + state // LOCAL
        for row in range(groups * group):
            contracted[
                row // group,
                place * SLOT : (place + 1) * SLOT,
                row % group * lanes : (row % group + 1) * lanes,
            ] = product[row * SLOT : (row + 1) * SLOT, state * lanes : (state + 1) * lanes]

    def mix(step):
        product = jnp.dot(coupling[...], contracted[step], preferred_element_type=jnp.float32)
        product = product.astype(jnp.bfloat16)
        for part in range(group):
            start = (group * step + part) * states
            for bond in range(bonds):
                mixed[start : start + states, bond * lanes : (bond + 1) * lanes] = product[
                    bond * states : (bond + 1) * states, part * lanes : (part + 1) * lanes
                ]

    def finish(step):
        place = slice(group * step * states, group * (step + 1) * states)
        image[place, :] = SHRINK * jnp.dot(
            mixed[place, :], right[...], preferred_element_type=jnp.float32
        )

    mix(0)
    for step in range(groups):
        if step + 1 < groups:
            mix(step + 1)
        finish(step)


def column_sum(x):
    return jnp.sum(x, axis=0, keepdims=True)


def state_half(image, states, index):
    pieces = image.reshape(image.shape[0] // states, states, image.shape[1])
    return jnp.where(index == 0, pieces[:, : states // 2, :], pieces[:, states // 2 :, :])


def first_kernel(
    env, coupling, right, vector, direct_in, passed_in,
    image, image_rows, sums,
    wide, extended, contracted, mixed,
):
    rows = extended.shape[0] // 3
    states = vector.shape[0] // rows
    half = image.shape[0]
    for place, source in zip((rows,) + halo_places(rows), (vector, direct_in, passed_in)):
        wide[...] = source[...].astype(jnp.float32)

        def store(columns, piece, place=place):
            extended[pl.ds(place, rows), columns] = piece

        states_apart(wide, rows, states, store)
    apply_steps(env, coupling, right, extended, contracted, mixed, image)
    out = image[...]

    def store_rows(columns, piece):
        image_rows[:, columns] = piece

    states_apart(image, half // states, states, store_rows)
    start = pl.multiple_of(lax.axis_index("mpo") * half, half)
    own = vector[pl.ds(start, half), :].astype(jnp.float32)
    lanes = out.shape[1]
    sums[...] = jnp.concatenate(
        [column_sum(own * own), column_sum(own * out), column_sum(out * out)]
        + [jnp.zeros((5, lanes), jnp.float32)],
        axis=0,
    )


def second_kernel(
    env, coupling, right, mine_in, other_in, direct_in, passed_in, first, vector, sums,
    image, sent, totals,
    extended, contracted, mixed,
):
    rows = direct_in.shape[0]
    part = rows // 2
    half = first.shape[0]
    core = lax.axis_index("mpo")
    direct, passed = halo_places(rows)
    mine = pl.multiple_of(rows + core * part, part)
    other = pl.multiple_of(rows + (1 - core) * part, part)
    extended[pl.ds(mine, part), :] = mine_in[...]
    extended[pl.ds(other, part), :] = other_in[...]
    extended[pl.ds(direct, rows), :] = direct_in[...]
    extended[pl.ds(passed, rows), :] = passed_in[...]
    apply_steps(env, coupling, right, extended, contracted, mixed, image)
    out = image[...]
    states = half // part
    sent[0:part] = state_half(first[...], states, 1 - core)
    sent[part : 2 * part] = state_half(out, states, 1 - core)
    own = vector[pl.ds(pl.multiple_of(core * half, half), half), :].astype(jnp.float32)
    lanes = out.shape[1]
    columns = jnp.concatenate(
        [sums[0:3, :], column_sum(own * out), column_sum(first[...] * out)]
        + [jnp.zeros((3, lanes), jnp.float32)],
        axis=0,
    )
    totals[...] = jnp.broadcast_to(columns[None], totals.shape)


def final_kernel(
    entries, first, second, got, vector, gathered,
    image_two, basis_two, projected,
):
    half = got.shape[0] // 2
    half_states = got.shape[1]
    states = 2 * half_states
    lanes = first.shape[1]
    core = lax.axis_index("mpo")
    totals = jnp.sum(jnp.sum(gathered[...], axis=0), axis=1, keepdims=True)
    s_aa, s_ay, s_yy, s_az, s_yz = (totals[i : i + 1, :] for i in range(5))
    scale_sq = s_aa / entries + EPSILON
    shrunk = s_ay / entries / scale_sq
    residual_sq = jnp.maximum(s_yy - 2.0 * shrunk * s_ay + shrunk * shrunk * s_aa, 0.0)
    residual_norm = jnp.sqrt(residual_sq / scale_sq / entries * (GROW * GROW) + EPSILON)
    factor = GROW / (jnp.sqrt(scale_sq) * residual_norm)
    final = (s_yz - shrunk * s_yy - shrunk * s_az + shrunk * shrunk * s_ay) / entries
    gamma = final * factor * factor * GROW
    r = lax.broadcasted_iota(jnp.int32, projected.shape, 0)
    c = lax.broadcasted_iota(jnp.int32, projected.shape, 1)
    diagonal = jnp.where(r == 0, shrunk * GROW, gamma)
    projected[...] = jnp.where(r == c, diagonal, residual_norm)

    size = half * half_states
    own = state_half(vector[...].astype(jnp.float32), states, core).reshape(2 * size, lanes)
    ours = jnp.where(core == 0, own[:size, :], own[size:, :])
    theirs = jnp.where(core == 0, own[size:, :], own[:size, :])
    mine = [state_half(image[...], states, core) for image in (first, second)]
    for index, (y, z), a in (
        (core, mine, ours),
        (1 - core, (got[0:half], got[half : 2 * half]), theirs),
    ):
        y = y.reshape(size, lanes)
        z = z.reshape(size, lanes)
        place = pl.ds(pl.multiple_of(index * size, size), size)
        basis_two[place, :] = ((y - shrunk * a) * factor).astype(jnp.bfloat16)
        image_two[place, :] = ((z - shrunk * y) * (factor * GROW)).astype(jnp.bfloat16)


def call(kernel, operands, outs, scratch, name, cost=None):
    return pl.pallas_call(
        kernel,
        out_shape=tuple(jax.ShapeDtypeStruct(shape, dtype) for shape, dtype in outs),
        in_specs=[WHOLE] * len(operands),
        out_specs=(WHOLE,) * len(outs),
        scratch_shapes=[pltpu.VMEM(shape, dtype) for shape, dtype in scratch],
        cost_estimate=cost,
        compiler_params=pltpu.CompilerParams(vmem_limit_bytes=VMEM_LIMIT),
        name=name,
    )(*operands)


def per_device(amplitudes, left_env, right_env, mpo_left, mpo_right, sector_table):
    rows, states, columns = amplitudes.shape
    band = left_env.shape[2]
    bonds = mpo_left.shape[0]
    half = rows // 2
    half_states = states // 2
    size = half * states
    block = lax.axis_index("brow")
    core = lax.axis_index("mpo")
    axes = ("brow", "bcol", "mpo")
    peers = lax.axis_size(axes)
    entries = float(rows * lax.axis_size("brow") * states * columns * lax.axis_size("bcol"))
    f32, bf16 = jnp.float32, jnp.bfloat16
    flat = amplitudes.reshape(rows * states, columns)

    env_there = swap_cores(left_env)
    direct_one = swap_blocks(flat)

    outside = jnp.full((rows,), -1, dtype=jnp.int32)
    padded = jnp.concatenate([outside, sector_table, outside])
    own_labels = lax.dynamic_slice_in_dim(padded, (block + 1) * rows + core * half, half, 0)
    partner = lax.dynamic_slice_in_dim(padded, block * rows, 3 * rows, 0)
    mask = (own_labels[:, None] == partner[None, :]).astype(f32)
    both = jnp.concatenate([mpo_left, mpo_right], axis=0)
    both = jnp.transpose(both, (0, 2, 3, 1)).reshape(2 * bonds * states, bonds)
    env, coupling = call(
        prepare_kernel,
        (left_env, env_there, mask, both),
        (
            ((half * SLOT, band), bf16),
            ((bonds * states, states * SLOT), bf16),
        ),
        (
            ((-(-band // 128) * SLOT * half, 128), f32),
            ((SLOT * states, 128), f32),
            ((SLOT * states, 128), f32),
            ((states * SLOT, 128), f32),
            ((states * SLOT, SLOT), f32),
            ((states // LOCAL * SLOT * states, 128), f32),
        ),
        "operands",
        cost=pl.CostEstimate(flops=4 * 10**9, bytes_accessed=2**23, transcendentals=0),
    )
    direct_one, env, coupling = lax.optimization_barrier((direct_one, env, coupling))
    passed_one = swap_cores(direct_one)
    right = right_env.reshape(bonds * columns, columns)

    work = (
        ((3 * rows, states * columns), bf16),
        ((half // GROUP, states * SLOT, GROUP * columns), bf16),
        ((size, bonds * columns), bf16),
    )
    first, first_rows, sums = call(
        first_kernel,
        (env, coupling, right, flat, direct_one, passed_one),
        (
            ((size, columns), f32),
            ((half, states * columns), bf16),
            ((8, columns), f32),
        ),
        (((rows * states, columns), f32),) + work,
        "first_image",
    )

    other_rows = swap_cores(first_rows)
    mine_first = core == 0
    block_rows = jnp.concatenate(
        [jnp.where(mine_first, first_rows, other_rows), jnp.where(mine_first, other_rows, first_rows)],
        axis=0,
    )
    direct_two = swap_blocks(block_rows)
    passed_two = swap_cores(direct_two)

    second, sent, totals = call(
        second_kernel,
        (env, coupling, right, first_rows, other_rows, direct_two, passed_two, first, flat, sums),
        (
            ((size, columns), f32),
            ((2 * half, half_states, columns), f32),
            ((peers, 8, columns), f32),
        ),
        work,
        "second_image",
    )
    got = swap_cores(sent)
    gathered = lax.all_to_all(totals, axes, 0, 0)

    def finish(*refs):
        final_kernel(entries, *refs)

    image_two, basis_two, projected = call(
        finish,
        (first, second, got, flat, gathered),
        (
            ((rows * half_states, columns), bf16),
            ((rows * half_states, columns), bf16),
            ((2, 2), f32),
        ),
        (),
        "outputs",
    )
    shape = (rows, half_states, columns)
    return (image_two.reshape(shape), basis_two.reshape(shape), projected)


def solution(mesh):
    return jax.shard_map(
        per_device,
        mesh=mesh,
        in_specs=(
            P(("groups", "brow"), None, "bcol"),
            P(("groups", "mpo"), "brow", None),
            P("groups", "bcol", None),
            P(),
            P(),
            P("groups"),
        ),
        out_specs=(
            P(("groups", "brow"), "mpo", "bcol"),
            P(("groups", "brow"), "mpo", "bcol"),
            P("groups", None),
        ),
        check_vma=False,
    )
```

```python
import jax
import jax.numpy as jnp
from jax import lax
from jax.experimental import pallas as pl
from jax.experimental.pallas import tpu as pltpu
from jax.sharding import PartitionSpec as P

EPSILON = 1e-06
SHRINK = 2.0**-12
GROW = 1.0 / SHRINK
SLOT = 32
LOCAL = 4
GROUP = 8
VMEM_LIMIT = 40 * 2**20
WHOLE = pl.BlockSpec(memory_space=pltpu.VMEM)


def swap_cores(x):
    return lax.ppermute(x, "mpo", [(0, 1), (1, 0)])


def neighbours(blocks, odd):
    pairs = []
    for i in range(blocks):
        partner = (i + 1 if i % 2 else i - 1) if odd else i ^ 1
        if 0 <= partner < blocks:
            pairs.append((i, partner))
    return pairs


def swap_blocks(x):
    blocks = lax.axis_size("brow")
    pairs = [
        (2 * i + core, 2 * j + core) for core in range(2) for i, j in neighbours(blocks, core == 1)
    ]
    return lax.ppermute(x, ("brow", "mpo"), pairs)


def halo_places(rows):
    even = lax.rem(lax.axis_index("brow") + lax.axis_index("mpo"), 2) == 0
    direct = jnp.where(even, 2 * rows, 0)
    return pl.multiple_of(direct, rows), pl.multiple_of(2 * rows - direct, rows)


def states_apart(wide, rows, states, store):
    lanes = wide.shape[1]
    for state in range(states):
        piece = wide[pl.ds(state, rows, stride=states), :].astype(jnp.bfloat16)
        store(slice(state * lanes, (state + 1) * lanes), piece)


def prepare_kernel(
    env_mine, env_there, mask, both_mpo,
    env, coupling,
    by_bond, left_pad, right_pad, left_rows, right_rows, spread,
):
    core = lax.axis_index("mpo")
    share, rows, _ = env_mine.shape
    half = rows // 2
    here = pl.ds(pl.multiple_of(core * half, half), half)
    part = SLOT // 2
    used, bonds = both_mpo.shape[0] // 2, both_mpo.shape[1]
    states = used // bonds
    left_pad[...] = jnp.zeros_like(left_pad)
    right_pad[...] = jnp.zeros_like(right_pad)
    left_pad[0:used, 0:bonds] = both_mpo[0:used, :]
    right_pad[0:used, 0:bonds] = both_mpo[used : 2 * used, :]
    for state in range(states):
        for group, owner in enumerate((core, 1 - core)):
            start = state * SLOT + group * part
            left_rows[start : start + part, :] = left_pad[
                pl.ds(owner * (share * states) + state, part, stride=states), :
            ]
        across = right_pad[pl.ds(state, SLOT, stride=states), :]
        right_rows[state * SLOT : (state + 1) * SLOT, :] = jnp.transpose(across)[0:SLOT, :]
    joined = lax.dot_general(
        right_rows[...],
        left_rows[:, 0:SLOT],
        (((1,), (1,)), ((), ())),
        precision=lax.Precision.HIGHEST,
        preferred_element_type=jnp.float32,
    )
    width = LOCAL * SLOT
    for i in range(LOCAL):
        for j in range(LOCAL):
            for inner in range(LOCAL):
                start = inner * SLOT * states + i * LOCAL + j
                spread[pl.ds(start, SLOT, stride=states), :] = joined[
                    (j * LOCAL + inner) * SLOT : (j * LOCAL + inner + 1) * SLOT,
                    i * width : (i + 1) * width,
                ]
    for inner in range(LOCAL):
        start = inner * SLOT * states
        coupling[:, inner * width : (inner + 1) * width] = spread[
            start : start + used, :
        ].astype(jnp.bfloat16)

    band = mask.shape[1]
    by_bond[...] = jnp.zeros_like(by_bond)
    for low in range(0, band, 128):
        width = min(128, band - low)
        base = low // 128 * SLOT * half
        for group, source in enumerate((env_mine, env_there)):
            for bond in range(share):
                start = base + (group * part + bond) * half
                piece = source[bond, here, low : low + width].astype(jnp.float32)
                by_bond[start : start + half, 0:width] = piece
        for row in range(half):
            piece = by_bond[pl.ds(base + row, SLOT, stride=half), :][:, 0:width]
            kept = jnp.where(mask[row : row + 1, low : low + width] > 0.0, piece, 0.0)
            env[row * SLOT : (row + 1) * SLOT, low : low + width] = kept.astype(jnp.bfloat16)


def apply_steps(env, coupling, right, extended, contracted, mixed, image):
    groups, depth, width = contracted.shape
    lanes = right.shape[1]
    group = width // lanes
    states = depth // SLOT
    bonds = mixed.shape[1] // lanes
    product = jnp.dot(env[...], extended[...], preferred_element_type=jnp.float32)
    product = product.astype(jnp.bfloat16)
    for state in range(states):
        place = state % LOCAL * LOCAL + state // LOCAL
        for row in range(groups * group):
            contracted[
                row // group,
                place * SLOT : (place + 1) * SLOT,
                row % group * lanes : (row % group + 1) * lanes,
            ] = product[row * SLOT : (row + 1) * SLOT, state * lanes : (state + 1) * lanes]

    def mix(step):
        product = jnp.dot(coupling[...], contracted[step], preferred_element_type=jnp.float32)
        product = product.astype(jnp.bfloat16)
        for part in range(group):
            start = (group * step + part) * states
            for bond in range(bonds):
                mixed[start : start + states, bond * lanes : (bond + 1) * lanes] = product[
                    bond * states : (bond + 1) * states, part * lanes : (part + 1) * lanes
                ]

    def finish(step):
        place = slice(group * step * states, group * (step + 1) * states)
        image[place, :] = SHRINK * jnp.dot(
            mixed[place, :], right[...], preferred_element_type=jnp.float32
        )

    mix(0)
    for step in range(groups):
        if step + 1 < groups:
            mix(step + 1)
        finish(step)


def column_sum(x):
    return jnp.sum(x, axis=0, keepdims=True)


def state_half(image, states, index):
    pieces = image.reshape(image.shape[0] // states, states, image.shape[1])
    return jnp.where(index == 0, pieces[:, : states // 2, :], pieces[:, states // 2 :, :])


def first_kernel(
    env, coupling, right, vector, direct_in, passed_in,
    image, image_rows, sums,
    wide, extended, contracted, mixed,
):
    rows = extended.shape[0] // 3
    states = vector.shape[0] // rows
    half = image.shape[0]
    for place, source in zip((rows,) + halo_places(rows), (vector, direct_in, passed_in)):
        wide[...] = source[...].astype(jnp.float32)

        def store(columns, piece, place=place):
            extended[pl.ds(place, rows), columns] = piece

        states_apart(wide, rows, states, store)
    apply_steps(env, coupling, right, extended, contracted, mixed, image)
    out = image[...]

    def store_rows(columns, piece):
        image_rows[:, columns] = piece

    states_apart(image, half // states, states, store_rows)
    start = pl.multiple_of(lax.axis_index("mpo") * half, half)
    own = vector[pl.ds(start, half), :].astype(jnp.float32)
    lanes = out.shape[1]
    sums[...] = jnp.concatenate(
        [column_sum(own * own), column_sum(own * out), column_sum(out * out)]
        + [jnp.zeros((5, lanes), jnp.float32)],
        axis=0,
    )


def second_kernel(
    env, coupling, right, own_here, own_there, even_here, even_there, odd_here, odd_there,
    first, vector, sums,
    image, sent, totals,
    extended, contracted, mixed,
):
    part = own_here.shape[0]
    rows = 2 * part
    half = first.shape[0]
    core = lax.axis_index("mpo")
    even = lax.rem(lax.axis_index("brow"), 2) == 0
    above, below = jnp.where(even, 2 * rows, 0), jnp.where(even, 0, 2 * rows)
    for base, here, there in (
        (rows, own_here, own_there), (above, even_here, even_there), (below, odd_here, odd_there)
    ):
        extended[pl.ds(pl.multiple_of(base + core * part, part), part), :] = here[...]
        extended[pl.ds(pl.multiple_of(base + (1 - core) * part, part), part), :] = there[...]
    apply_steps(env, coupling, right, extended, contracted, mixed, image)
    out = image[...]
    states = half // part
    sent[0:part] = state_half(first[...], states, 1 - core)
    sent[part : 2 * part] = state_half(out, states, 1 - core)
    own = vector[pl.ds(pl.multiple_of(core * half, half), half), :].astype(jnp.float32)
    lanes = out.shape[1]
    columns = jnp.concatenate(
        [sums[0:3, :], column_sum(own * out), column_sum(first[...] * out)]
        + [jnp.zeros((3, lanes), jnp.float32)],
        axis=0,
    )
    lane = lax.broadcasted_iota(jnp.int32, columns.shape, 1)
    row = lax.broadcasted_iota(jnp.int32, columns.shape, 0)
    spread = jnp.where(lane == row, jnp.sum(columns, axis=1, keepdims=True), 0.0)
    totals[...] = jnp.broadcast_to(column_sum(spread)[None], totals.shape)


def final_kernel(
    entries, first, second, got, vector, gathered,
    image_two, basis_two, projected,
):
    half = got.shape[0] // 2
    half_states = got.shape[1]
    states = 2 * half_states
    lanes = first.shape[1]
    core = lax.axis_index("mpo")
    totals = jnp.sum(gathered[...], axis=0)
    lane = lax.broadcasted_iota(jnp.int32, totals.shape, 1)
    s_aa, s_ay, s_yy, s_az, s_yz = (
        jnp.sum(jnp.where(lane == i, totals, 0.0), axis=1, keepdims=True) for i in range(5)
    )
    scale_sq = s_aa / entries + EPSILON
    shrunk = s_ay / entries / scale_sq
    residual_sq = jnp.maximum(s_yy - 2.0 * shrunk * s_ay + shrunk * shrunk * s_aa, 0.0)
    residual_norm = jnp.sqrt(residual_sq / scale_sq / entries * (GROW * GROW) + EPSILON)
    factor = GROW / (jnp.sqrt(scale_sq) * residual_norm)
    final = (s_yz - shrunk * s_yy - shrunk * s_az + shrunk * shrunk * s_ay) / entries
    gamma = final * factor * factor * GROW
    r = lax.broadcasted_iota(jnp.int32, projected.shape, 0)
    c = lax.broadcasted_iota(jnp.int32, projected.shape, 1)
    diagonal = jnp.where(r == 0, shrunk * GROW, gamma)
    projected[...] = jnp.where(r == c, diagonal, residual_norm)

    size = half * half_states
    own = state_half(vector[...].astype(jnp.float32), states, core).reshape(2 * size, lanes)
    ours = jnp.where(core == 0, own[:size, :], own[size:, :])
    theirs = jnp.where(core == 0, own[size:, :], own[:size, :])
    mine = [state_half(image[...], states, core) for image in (first, second)]
    for index, (y, z), a in (
        (core, mine, ours),
        (1 - core, (got[0:half], got[half : 2 * half]), theirs),
    ):
        y = y.reshape(size, lanes)
        z = z.reshape(size, lanes)
        place = pl.ds(pl.multiple_of(index * size, size), size)
        basis_two[place, :] = ((y - shrunk * a) * factor).astype(jnp.bfloat16)
        image_two[place, :] = ((z - shrunk * y) * (factor * GROW)).astype(jnp.bfloat16)


def call(kernel, operands, outs, scratch, name, cost=None):
    return pl.pallas_call(
        kernel,
        out_shape=tuple(jax.ShapeDtypeStruct(shape, dtype) for shape, dtype in outs),
        in_specs=[WHOLE] * len(operands),
        out_specs=(WHOLE,) * len(outs),
        scratch_shapes=[pltpu.VMEM(shape, dtype) for shape, dtype in scratch],
        cost_estimate=cost,
        compiler_params=pltpu.CompilerParams(vmem_limit_bytes=VMEM_LIMIT),
        name=name,
    )(*operands)


def per_device(amplitudes, left_env, right_env, mpo_left, mpo_right, sector_table):
    rows, states, columns = amplitudes.shape
    band = left_env.shape[2]
    bonds = mpo_left.shape[0]
    half = rows // 2
    half_states = states // 2
    size = half * states
    block = lax.axis_index("brow")
    core = lax.axis_index("mpo")
    axes = ("brow", "bcol", "mpo")
    peers = lax.axis_size(axes)
    entries = float(rows * lax.axis_size("brow") * states * columns * lax.axis_size("bcol"))
    f32, bf16 = jnp.float32, jnp.bfloat16
    flat = amplitudes.reshape(rows * states, columns)

    env_there = swap_cores(left_env)
    direct_one = swap_blocks(flat)

    outside = jnp.full((rows,), -1, dtype=jnp.int32)
    padded = jnp.concatenate([outside, sector_table, outside])
    own_labels = lax.dynamic_slice_in_dim(padded, (block + 1) * rows + core * half, half, 0)
    partner = lax.dynamic_slice_in_dim(padded, block * rows, 3 * rows, 0)
    mask = (own_labels[:, None] == partner[None, :]).astype(f32)
    both = jnp.concatenate([mpo_left, mpo_right], axis=0)
    both = jnp.transpose(both, (0, 2, 3, 1)).reshape(2 * bonds * states, bonds)
    env, coupling = call(
        prepare_kernel,
        (left_env, env_there, mask, both),
        (
            ((half * SLOT, band), bf16),
            ((bonds * states, states * SLOT), bf16),
        ),
        (
            ((-(-band // 128) * SLOT * half, 128), f32),
            ((SLOT * states, 128), f32),
            ((SLOT * states, 128), f32),
            ((states * SLOT, 128), f32),
            ((states * SLOT, SLOT), f32),
            ((states // LOCAL * SLOT * states, 128), f32),
        ),
        "operands",
        cost=pl.CostEstimate(flops=4 * 10**9, bytes_accessed=2**23, transcendentals=0),
    )
    direct_one, env, coupling = lax.optimization_barrier((direct_one, env, coupling))
    passed_one = swap_cores(direct_one)
    right = right_env.reshape(bonds * columns, columns)

    work = (
        ((3 * rows, states * columns), bf16),
        ((half // GROUP, states * SLOT, GROUP * columns), bf16),
        ((size, bonds * columns), bf16),
    )
    first, first_rows, sums = call(
        first_kernel,
        (env, coupling, right, flat, direct_one, passed_one),
        (
            ((size, columns), f32),
            ((half, states * columns), bf16),
            ((8, columns), f32),
        ),
        (((rows * states, columns), f32),) + work,
        "first_image",
    )

    blocks = lax.axis_size("brow")
    even_rows = lax.ppermute(first_rows, "brow", neighbours(blocks, False))
    odd_rows = lax.ppermute(first_rows, "brow", neighbours(blocks, True))
    pieces = [(x, swap_cores(x)) for x in (first_rows, even_rows, odd_rows)]
    pieces = [x for pair in pieces for x in pair]

    second, sent, totals = call(
        second_kernel,
        (env, coupling, right, *pieces, first, flat, sums),
        (
            ((size, columns), f32),
            ((2 * half, half_states, columns), f32),
            ((peers, 1, columns), f32),
        ),
        work,
        "second_image",
    )
    got = swap_cores(sent)
    gathered = lax.all_to_all(totals, axes, 0, 0)

    def finish(*refs):
        final_kernel(entries, *refs)

    image_two, basis_two, projected = call(
        finish,
        (first, second, got, flat, gathered),
        (
            ((rows * half_states, columns), bf16),
            ((rows * half_states, columns), bf16),
            ((2, 2), f32),
        ),
        (),
        "outputs",
    )
    shape = (rows, half_states, columns)
    return (image_two.reshape(shape), basis_two.reshape(shape), projected)


def solution(mesh):
    return jax.shard_map(
        per_device,
        mesh=mesh,
        in_specs=(
            P(("groups", "brow"), None, "bcol"),
            P(("groups", "mpo"), "brow", None),
            P("groups", "bcol", None),
            P(),
            P(),
            P("groups"),
        ),
        out_specs=(
            P(("groups", "brow"), "mpo", "bcol"),
            P(("groups", "brow"), "mpo", "bcol"),
            P("groups", None),
        ),
        check_vma=False,
    )
```

```python
import jax
import jax.numpy as jnp
from jax import lax
from jax.experimental import pallas as pl
from jax.experimental.pallas import tpu as pltpu
from jax.sharding import PartitionSpec as P

EPSILON = 1e-06
SHRINK = 2.0**-12
GROW = 1.0 / SHRINK
SLOT = 32
LOCAL = 4
GROUP = 8
VMEM_LIMIT = 40 * 2**20
SHORT = pl.CostEstimate(flops=10**9, bytes_accessed=2**21, transcendentals=0)
WHOLE = pl.BlockSpec(memory_space=pltpu.VMEM)


def swap_cores(x):
    return lax.ppermute(x, "mpo", [(0, 1), (1, 0)])


def neighbours(blocks, odd):
    pairs = []
    for i in range(blocks):
        partner = (i + 1 if i % 2 else i - 1) if odd else i ^ 1
        if 0 <= partner < blocks:
            pairs.append((i, partner))
    return pairs


def swap_blocks(x):
    blocks = lax.axis_size("brow")
    pairs = [
        (2 * i + core, 2 * j + core) for core in range(2) for i, j in neighbours(blocks, core == 1)
    ]
    return lax.ppermute(x, ("brow", "mpo"), pairs)


def halo_places(rows):
    even = lax.rem(lax.axis_index("brow") + lax.axis_index("mpo"), 2) == 0
    direct = jnp.where(even, 2 * rows, 0)
    return pl.multiple_of(direct, rows), pl.multiple_of(2 * rows - direct, rows)


def states_apart(wide, rows, states, store):
    lanes = wide.shape[1]
    for state in range(states):
        piece = wide[pl.ds(state, rows, stride=states), :].astype(jnp.bfloat16)
        store(slice(state * lanes, (state + 1) * lanes), piece)


def prepare_kernel(
    env_mine, env_there, mask, both_mpo,
    env, coupling,
    by_bond, left_pad, right_pad, left_rows, right_rows, spread,
):
    core = lax.axis_index("mpo")
    share, rows, _ = env_mine.shape
    half = rows // 2
    here = pl.ds(pl.multiple_of(core * half, half), half)
    part = SLOT // 2
    used, bonds = both_mpo.shape[0] // 2, both_mpo.shape[1]
    states = used // bonds
    left_pad[...] = jnp.zeros_like(left_pad)
    right_pad[...] = jnp.zeros_like(right_pad)
    left_pad[0:used, 0:bonds] = both_mpo[0:used, :]
    right_pad[0:used, 0:bonds] = both_mpo[used : 2 * used, :]
    for state in range(states):
        for group, owner in enumerate((core, 1 - core)):
            start = state * SLOT + group * part
            left_rows[start : start + part, :] = left_pad[
                pl.ds(owner * (share * states) + state, part, stride=states), :
            ]
        across = right_pad[pl.ds(state, SLOT, stride=states), :]
        right_rows[state * SLOT : (state + 1) * SLOT, :] = jnp.transpose(across)[0:SLOT, :]
    joined = lax.dot_general(
        right_rows[...],
        left_rows[:, 0:SLOT],
        (((1,), (1,)), ((), ())),
        precision=lax.Precision.HIGHEST,
        preferred_element_type=jnp.float32,
    )
    width = LOCAL * SLOT
    for i in range(LOCAL):
        for j in range(LOCAL):
            for inner in range(LOCAL):
                start = inner * SLOT * states + i * LOCAL + j
                spread[pl.ds(start, SLOT, stride=states), :] = joined[
                    (j * LOCAL + inner) * SLOT : (j * LOCAL + inner + 1) * SLOT,
                    i * width : (i + 1) * width,
                ]
    for inner in range(LOCAL):
        start = inner * SLOT * states
        coupling[:, inner * width : (inner + 1) * width] = spread[
            start : start + used, :
        ].astype(jnp.bfloat16)

    band = mask.shape[1]
    by_bond[...] = jnp.zeros_like(by_bond)
    for low in range(0, band, 128):
        width = min(128, band - low)
        base = low // 128 * SLOT * half
        for group, source in enumerate((env_mine, env_there)):
            for bond in range(share):
                start = base + (group * part + bond) * half
                piece = source[bond, here, low : low + width].astype(jnp.float32)
                by_bond[start : start + half, 0:width] = piece
        for row in range(half):
            piece = by_bond[pl.ds(base + row, SLOT, stride=half), :][:, 0:width]
            kept = jnp.where(mask[row : row + 1, low : low + width] > 0.0, piece, 0.0)
            env[row * SLOT : (row + 1) * SLOT, low : low + width] = kept.astype(jnp.bfloat16)


def apply_steps(env, coupling, right, extended, contracted, mixed, image):
    groups, depth, width = contracted.shape
    lanes = right.shape[1]
    group = width // lanes
    states = depth // SLOT
    bonds = mixed.shape[1] // lanes
    product = jnp.dot(env[...], extended[...], preferred_element_type=jnp.float32)
    product = product.astype(jnp.bfloat16)
    for state in range(states):
        place = state % LOCAL * LOCAL + state // LOCAL
        for row in range(groups * group):
            contracted[
                row // group,
                place * SLOT : (place + 1) * SLOT,
                row % group * lanes : (row % group + 1) * lanes,
            ] = product[row * SLOT : (row + 1) * SLOT, state * lanes : (state + 1) * lanes]

    def mix(step):
        product = jnp.dot(coupling[...], contracted[step], preferred_element_type=jnp.float32)
        product = product.astype(jnp.bfloat16)
        for part in range(group):
            start = (group * step + part) * states
            for bond in range(bonds):
                mixed[start : start + states, bond * lanes : (bond + 1) * lanes] = product[
                    bond * states : (bond + 1) * states, part * lanes : (part + 1) * lanes
                ]

    def finish(step):
        place = slice(group * step * states, group * (step + 1) * states)
        image[place, :] = SHRINK * jnp.dot(
            mixed[place, :], right[...], preferred_element_type=jnp.float32
        )

    mix(0)
    for step in range(groups):
        if step + 1 < groups:
            mix(step + 1)
        finish(step)


def column_sum(x):
    return jnp.sum(x, axis=0, keepdims=True)


def state_half(image, states, index):
    pieces = image.reshape(image.shape[0] // states, states, image.shape[1])
    return jnp.where(index == 0, pieces[:, : states // 2, :], pieces[:, states // 2 :, :])


def lay_kernel(vector, direct, vector_rows, direct_rows, wide):
    rows, width = vector_rows.shape
    states = width // vector.shape[1]
    for source, target in ((vector, vector_rows), (direct, direct_rows)):
        wide[...] = source[...].astype(jnp.float32)

        def store(columns, piece, target=target):
            target[:, columns] = piece

        states_apart(wide, rows, states, store)


def first_kernel(
    env, coupling, right, vector_rows, direct_rows, passed_in,
    image, image_rows,
    wide, extended, contracted, mixed,
):
    rows = vector_rows.shape[0]
    states = passed_in.shape[0] // rows
    half = image.shape[0]
    direct, passed = halo_places(rows)
    extended[rows : 2 * rows, :] = vector_rows[...]
    extended[pl.ds(direct, rows), :] = direct_rows[...]
    wide[...] = passed_in[...].astype(jnp.float32)

    def store(columns, piece):
        extended[pl.ds(passed, rows), columns] = piece

    states_apart(wide, rows, states, store)
    apply_steps(env, coupling, right, extended, contracted, mixed, image)

    def store_rows(columns, piece):
        image_rows[:, columns] = piece

    states_apart(image, half // states, states, store_rows)


def sums_kernel(image, vector, sums):
    half, lanes = image.shape
    start = pl.multiple_of(lax.axis_index("mpo") * half, half)
    own = vector[pl.ds(start, half), :].astype(jnp.float32)
    out = image[...]
    sums[...] = jnp.concatenate(
        [column_sum(own * own), column_sum(own * out), column_sum(out * out)]
        + [jnp.zeros((5, lanes), jnp.float32)],
        axis=0,
    )


def second_kernel(
    env, coupling, right, own_here, own_there, even_here, even_there, odd_here, odd_there,
    first, vector, sums,
    image, sent, totals,
    extended, contracted, mixed,
):
    part = own_here.shape[0]
    rows = 2 * part
    half = first.shape[0]
    core = lax.axis_index("mpo")
    even = lax.rem(lax.axis_index("brow"), 2) == 0
    above, below = jnp.where(even, 2 * rows, 0), jnp.where(even, 0, 2 * rows)
    for base, here, there in (
        (rows, own_here, own_there), (above, even_here, even_there), (below, odd_here, odd_there)
    ):
        extended[pl.ds(pl.multiple_of(base + core * part, part), part), :] = here[...]
        extended[pl.ds(pl.multiple_of(base + (1 - core) * part, part), part), :] = there[...]
    apply_steps(env, coupling, right, extended, contracted, mixed, image)
    out = image[...]
    states = half // part
    sent[0:part] = state_half(first[...], states, 1 - core)
    sent[part : 2 * part] = state_half(out, states, 1 - core)
    own = vector[pl.ds(pl.multiple_of(core * half, half), half), :].astype(jnp.float32)
    lanes = out.shape[1]
    columns = jnp.concatenate(
        [sums[0:3, :], column_sum(own * out), column_sum(first[...] * out)]
        + [jnp.zeros((3, lanes), jnp.float32)],
        axis=0,
    )
    lane = lax.broadcasted_iota(jnp.int32, columns.shape, 1)
    row = lax.broadcasted_iota(jnp.int32, columns.shape, 0)
    spread = jnp.where(lane == row, jnp.sum(columns, axis=1, keepdims=True), 0.0)
    totals[...] = jnp.broadcast_to(column_sum(spread)[None], totals.shape)


def final_kernel(
    entries, first, second, got, vector, gathered,
    image_two, basis_two, projected,
):
    half = got.shape[0] // 2
    half_states = got.shape[1]
    states = 2 * half_states
    lanes = first.shape[1]
    core = lax.axis_index("mpo")
    totals = jnp.sum(gathered[...], axis=0)
    lane = lax.broadcasted_iota(jnp.int32, totals.shape, 1)
    s_aa, s_ay, s_yy, s_az, s_yz = (
        jnp.sum(jnp.where(lane == i, totals, 0.0), axis=1, keepdims=True) for i in range(5)
    )
    scale_sq = s_aa / entries + EPSILON
    shrunk = s_ay / entries / scale_sq
    residual_sq = jnp.maximum(s_yy - 2.0 * shrunk * s_ay + shrunk * shrunk * s_aa, 0.0)
    residual_norm = jnp.sqrt(residual_sq / scale_sq / entries * (GROW * GROW) + EPSILON)
    factor = GROW / (jnp.sqrt(scale_sq) * residual_norm)
    final = (s_yz - shrunk * s_yy - shrunk * s_az + shrunk * shrunk * s_ay) / entries
    gamma = final * factor * factor * GROW
    r = lax.broadcasted_iota(jnp.int32, projected.shape, 0)
    c = lax.broadcasted_iota(jnp.int32, projected.shape, 1)
    diagonal = jnp.where(r == 0, shrunk * GROW, gamma)
    projected[...] = jnp.where(r == c, diagonal, residual_norm)

    size = half * half_states
    own = state_half(vector[...].astype(jnp.float32), states, core).reshape(2 * size, lanes)
    ours = jnp.where(core == 0, own[:size, :], own[size:, :])
    theirs = jnp.where(core == 0, own[size:, :], own[:size, :])
    mine = [state_half(image[...], states, core) for image in (first, second)]
    for index, (y, z), a in (
        (core, mine, ours),
        (1 - core, (got[0:half], got[half : 2 * half]), theirs),
    ):
        y = y.reshape(size, lanes)
        z = z.reshape(size, lanes)
        place = pl.ds(pl.multiple_of(index * size, size), size)
        basis_two[place, :] = ((y - shrunk * a) * factor).astype(jnp.bfloat16)
        image_two[place, :] = ((z - shrunk * y) * (factor * GROW)).astype(jnp.bfloat16)


def call(kernel, operands, outs, scratch, name, cost=None):
    return pl.pallas_call(
        kernel,
        out_shape=tuple(jax.ShapeDtypeStruct(shape, dtype) for shape, dtype in outs),
        in_specs=[WHOLE] * len(operands),
        out_specs=(WHOLE,) * len(outs),
        scratch_shapes=[pltpu.VMEM(shape, dtype) for shape, dtype in scratch],
        cost_estimate=cost,
        compiler_params=pltpu.CompilerParams(vmem_limit_bytes=VMEM_LIMIT),
        name=name,
    )(*operands)


def per_device(amplitudes, left_env, right_env, mpo_left, mpo_right, sector_table):
    rows, states, columns = amplitudes.shape
    band = left_env.shape[2]
    bonds = mpo_left.shape[0]
    half = rows // 2
    half_states = states // 2
    size = half * states
    block = lax.axis_index("brow")
    core = lax.axis_index("mpo")
    axes = ("brow", "bcol", "mpo")
    peers = lax.axis_size(axes)
    entries = float(rows * lax.axis_size("brow") * states * columns * lax.axis_size("bcol"))
    f32, bf16 = jnp.float32, jnp.bfloat16
    flat = amplitudes.reshape(rows * states, columns)

    env_there = swap_cores(left_env)
    direct_one = swap_blocks(flat)

    outside = jnp.full((rows,), -1, dtype=jnp.int32)
    padded = jnp.concatenate([outside, sector_table, outside])
    own_labels = lax.dynamic_slice_in_dim(padded, (block + 1) * rows + core * half, half, 0)
    partner = lax.dynamic_slice_in_dim(padded, block * rows, 3 * rows, 0)
    mask = (own_labels[:, None] == partner[None, :]).astype(f32)
    both = jnp.concatenate([mpo_left, mpo_right], axis=0)
    both = jnp.transpose(both, (0, 2, 3, 1)).reshape(2 * bonds * states, bonds)
    env, coupling = call(
        prepare_kernel,
        (left_env, env_there, mask, both),
        (
            ((half * SLOT, band), bf16),
            ((bonds * states, states * SLOT), bf16),
        ),
        (
            ((-(-band // 128) * SLOT * half, 128), f32),
            ((SLOT * states, 128), f32),
            ((SLOT * states, 128), f32),
            ((states * SLOT, 128), f32),
            ((states * SLOT, SLOT), f32),
            ((states // LOCAL * SLOT * states, 128), f32),
        ),
        "operands",
        cost=pl.CostEstimate(flops=4 * 10**9, bytes_accessed=2**23, transcendentals=0),
    )
    direct_one, env, coupling = lax.optimization_barrier((direct_one, env, coupling))
    passed_one = swap_cores(direct_one)
    right = right_env.reshape(bonds * columns, columns)

    work = (
        ((3 * rows, states * columns), bf16),
        ((half // GROUP, states * SLOT, GROUP * columns), bf16),
        ((size, bonds * columns), bf16),
    )
    laid = ((rows, states * columns), bf16)
    wide = ((rows * states, columns), f32)
    vector_rows, direct_rows = call(
        lay_kernel, (flat, direct_one), (laid, laid), (wide,), "rows", cost=SHORT
    )
    first, first_rows = call(
        first_kernel,
        (env, coupling, right, vector_rows, direct_rows, passed_one),
        (((size, columns), f32), ((half, states * columns), bf16)),
        (wide,) + work,
        "first_image",
    )
    (sums,) = call(sums_kernel, (first, flat), (((8, columns), f32),), (), "sums", cost=SHORT)

    blocks = lax.axis_size("brow")
    even_rows = lax.ppermute(first_rows, "brow", neighbours(blocks, False))
    odd_rows = lax.ppermute(first_rows, "brow", neighbours(blocks, True))
    pieces = [(x, swap_cores(x)) for x in (first_rows, even_rows, odd_rows)]
    pieces = [x for pair in pieces for x in pair]

    second, sent, totals = call(
        second_kernel,
        (env, coupling, right, *pieces, first, flat, sums),
        (
            ((size, columns), f32),
            ((2 * half, half_states, columns), f32),
            ((peers, 1, columns), f32),
        ),
        work,
        "second_image",
    )
    got = swap_cores(sent)
    gathered = lax.all_to_all(totals, axes, 0, 0)

    def finish(*refs):
        final_kernel(entries, *refs)

    image_two, basis_two, projected = call(
        finish,
        (first, second, got, flat, gathered),
        (
            ((rows * half_states, columns), bf16),
            ((rows * half_states, columns), bf16),
            ((2, 2), f32),
        ),
        (),
        "outputs",
    )
    shape = (rows, half_states, columns)
    return (image_two.reshape(shape), basis_two.reshape(shape), projected)


def solution(mesh):
    return jax.shard_map(
        per_device,
        mesh=mesh,
        in_specs=(
            P(("groups", "brow"), None, "bcol"),
            P(("groups", "mpo"), "brow", None),
            P("groups", "bcol", None),
            P(),
            P(),
            P("groups"),
        ),
        out_specs=(
            P(("groups", "brow"), "mpo", "bcol"),
            P(("groups", "brow"), "mpo", "bcol"),
            P("groups", None),
        ),
        check_vma=False,
    )
```

```python
import jax
import jax.numpy as jnp
from jax import lax
from jax.experimental import pallas as pl
from jax.experimental.pallas import tpu as pltpu
from jax.sharding import PartitionSpec as P

EPSILON = 1e-06
SHRINK = 2.0**-12
GROW = 1.0 / SHRINK
SLOT = 32
LOCAL = 4
GROUP = 8
VMEM_LIMIT = 40 * 2**20
SHORT = pl.CostEstimate(flops=10**9, bytes_accessed=2**21, transcendentals=0)
WHOLE = pl.BlockSpec(memory_space=pltpu.VMEM)


def swap_cores(x):
    return lax.ppermute(x, "mpo", [(0, 1), (1, 0)])


def partner_of(block, slab, odd):
    blocks, slabs = lax.axis_size("brow"), lax.axis_size("bcol")
    other = (block + 1 if block % 2 else block - 1) if odd else block ^ 1
    if 0 <= other < blocks:
        return other, slab
    return block, slab ^ 1 if slab ^ 1 < slabs else slab


def place_of(block, slab, core):
    return (block * lax.axis_size("bcol") + slab) * 2 + core


def trade(x, odd):
    pairs = []
    for block in range(lax.axis_size("brow")):
        for slab in range(lax.axis_size("bcol")):
            for core in range(2):
                other = partner_of(block, slab, odd[core])
                pairs.append((place_of(block, slab, core), place_of(*other, core)))
    return lax.ppermute(x, ("brow", "bcol", "mpo"), pairs)


def halo_places(rows):
    even = lax.rem(lax.axis_index("brow") + lax.axis_index("mpo"), 2) == 0
    direct = jnp.where(even, 2 * rows, 0)
    return pl.multiple_of(direct, rows), pl.multiple_of(2 * rows - direct, rows)


def states_apart(wide, rows, states, store):
    lanes = wide.shape[1]
    for state in range(states):
        piece = wide[pl.ds(state, rows, stride=states), :].astype(jnp.bfloat16)
        store(slice(state * lanes, (state + 1) * lanes), piece)


def prepare_kernel(
    env_mine, env_there, mask, both_mpo,
    env, coupling,
    by_bond, left_pad, right_pad, left_rows, right_rows, spread,
):
    core = lax.axis_index("mpo")
    share, rows, _ = env_mine.shape
    half = rows // 2
    here = pl.ds(pl.multiple_of(core * half, half), half)
    part = SLOT // 2
    used, bonds = both_mpo.shape[0] // 2, both_mpo.shape[1]
    states = used // bonds
    left_pad[...] = jnp.zeros_like(left_pad)
    right_pad[...] = jnp.zeros_like(right_pad)
    left_pad[0:used, 0:bonds] = both_mpo[0:used, :]
    right_pad[0:used, 0:bonds] = both_mpo[used : 2 * used, :]
    for state in range(states):
        for group, owner in enumerate((core, 1 - core)):
            start = state * SLOT + group * part
            left_rows[start : start + part, :] = left_pad[
                pl.ds(owner * (share * states) + state, part, stride=states), :
            ]
        across = right_pad[pl.ds(state, SLOT, stride=states), :]
        right_rows[state * SLOT : (state + 1) * SLOT, :] = jnp.transpose(across)[0:SLOT, :]
    joined = lax.dot_general(
        right_rows[...],
        left_rows[:, 0:SLOT],
        (((1,), (1,)), ((), ())),
        precision=lax.Precision.HIGHEST,
        preferred_element_type=jnp.float32,
    )
    width = LOCAL * SLOT
    for i in range(LOCAL):
        for j in range(LOCAL):
            for inner in range(LOCAL):
                start = inner * SLOT * states + i * LOCAL + j
                spread[pl.ds(start, SLOT, stride=states), :] = joined[
                    (j * LOCAL + inner) * SLOT : (j * LOCAL + inner + 1) * SLOT,
                    i * width : (i + 1) * width,
                ]
    for inner in range(LOCAL):
        start = inner * SLOT * states
        coupling[:, inner * width : (inner + 1) * width] = spread[
            start : start + used, :
        ].astype(jnp.bfloat16)

    band = mask.shape[1]
    by_bond[...] = jnp.zeros_like(by_bond)
    for low in range(0, band, 128):
        width = min(128, band - low)
        base = low // 128 * SLOT * half
        for group, source in enumerate((env_mine, env_there)):
            for bond in range(share):
                start = base + (group * part + bond) * half
                piece = source[bond, here, low : low + width].astype(jnp.float32)
                by_bond[start : start + half, 0:width] = piece
        for row in range(half):
            piece = by_bond[pl.ds(base + row, SLOT, stride=half), :][:, 0:width]
            kept = jnp.where(mask[row : row + 1, low : low + width] > 0.0, piece, 0.0)
            env[row * SLOT : (row + 1) * SLOT, low : low + width] = kept.astype(jnp.bfloat16)


def apply_steps(env, coupling, right, extended, contracted, mixed, image):
    groups, depth, width = contracted.shape
    lanes = right.shape[1]
    group = width // lanes
    states = depth // SLOT
    bonds = mixed.shape[1] // lanes
    product = jnp.dot(env[...], extended[...], preferred_element_type=jnp.float32)
    product = product.astype(jnp.bfloat16)
    for state in range(states):
        place = state % LOCAL * LOCAL + state // LOCAL
        for row in range(groups * group):
            contracted[
                row // group,
                place * SLOT : (place + 1) * SLOT,
                row % group * lanes : (row % group + 1) * lanes,
            ] = product[row * SLOT : (row + 1) * SLOT, state * lanes : (state + 1) * lanes]

    def mix(step):
        product = jnp.dot(coupling[...], contracted[step], preferred_element_type=jnp.float32)
        product = product.astype(jnp.bfloat16)
        for part in range(group):
            start = (group * step + part) * states
            for bond in range(bonds):
                mixed[start : start + states, bond * lanes : (bond + 1) * lanes] = product[
                    bond * states : (bond + 1) * states, part * lanes : (part + 1) * lanes
                ]

    def finish(step):
        place = slice(group * step * states, group * (step + 1) * states)
        image[place, :] = SHRINK * jnp.dot(
            mixed[place, :], right[...], preferred_element_type=jnp.float32
        )

    mix(0)
    for step in range(groups):
        if step + 1 < groups:
            mix(step + 1)
        finish(step)


def column_sum(x):
    return jnp.sum(x, axis=0, keepdims=True)


def state_half(image, states, index):
    pieces = image.reshape(image.shape[0] // states, states, image.shape[1])
    return jnp.where(index == 0, pieces[:, : states // 2, :], pieces[:, states // 2 :, :])


def lay_kernel(vector, direct, vector_rows, direct_rows, wide):
    rows, width = vector_rows.shape
    states = width // vector.shape[1]
    for source, target in ((vector, vector_rows), (direct, direct_rows)):
        wide[...] = source[...].astype(jnp.float32)

        def store(columns, piece, target=target):
            target[:, columns] = piece

        states_apart(wide, rows, states, store)


def first_kernel(
    env, coupling, right, vector_rows, direct_rows, passed_in,
    image, image_rows,
    wide, extended, contracted, mixed,
):
    rows = vector_rows.shape[0]
    states = passed_in.shape[0] // rows
    half = image.shape[0]
    direct, passed = halo_places(rows)
    extended[rows : 2 * rows, :] = vector_rows[...]
    extended[pl.ds(direct, rows), :] = direct_rows[...]
    wide[...] = passed_in[...].astype(jnp.float32)

    def store(columns, piece):
        extended[pl.ds(passed, rows), columns] = piece

    states_apart(wide, rows, states, store)
    apply_steps(env, coupling, right, extended, contracted, mixed, image)

    def store_rows(columns, piece):
        image_rows[:, columns] = piece

    states_apart(image, half // states, states, store_rows)


def sums_kernel(image, vector, sums):
    half, lanes = image.shape
    start = pl.multiple_of(lax.axis_index("mpo") * half, half)
    own = vector[pl.ds(start, half), :].astype(jnp.float32)
    out = image[...]
    sums[...] = jnp.concatenate(
        [column_sum(own * own), column_sum(own * out), column_sum(out * out)]
        + [jnp.zeros((5, lanes), jnp.float32)],
        axis=0,
    )


def second_kernel(
    env, coupling, right, own_here, own_there, even_here, even_there, odd_here, odd_there,
    first, vector, sums,
    image, sent, totals,
    extended, contracted, mixed,
):
    part = own_here.shape[0]
    rows = 2 * part
    half = first.shape[0]
    core = lax.axis_index("mpo")
    even = lax.rem(lax.axis_index("brow"), 2) == 0
    above, below = jnp.where(even, 2 * rows, 0), jnp.where(even, 0, 2 * rows)
    for base, here, there in (
        (rows, own_here, own_there), (above, even_here, even_there), (below, odd_here, odd_there)
    ):
        extended[pl.ds(pl.multiple_of(base + core * part, part), part), :] = here[...]
        extended[pl.ds(pl.multiple_of(base + (1 - core) * part, part), part), :] = there[...]
    apply_steps(env, coupling, right, extended, contracted, mixed, image)
    out = image[...]
    states = half // part
    sent[0:part] = state_half(first[...], states, 1 - core)
    sent[part : 2 * part] = state_half(out, states, 1 - core)
    own = vector[pl.ds(pl.multiple_of(core * half, half), half), :].astype(jnp.float32)
    lanes = out.shape[1]
    columns = jnp.concatenate(
        [sums[0:3, :], column_sum(own * out), column_sum(first[...] * out)]
        + [jnp.zeros((3, lanes), jnp.float32)],
        axis=0,
    )
    lane = lax.broadcasted_iota(jnp.int32, columns.shape, 1)
    row = lax.broadcasted_iota(jnp.int32, columns.shape, 0)
    spread = jnp.where(lane == row, jnp.sum(columns, axis=1, keepdims=True), 0.0)
    totals[...] = jnp.broadcast_to(column_sum(spread)[None], totals.shape)


def final_kernel(
    entries, first, second, got, vector, gathered,
    image_two, basis_two, projected,
):
    half = got.shape[0] // 2
    half_states = got.shape[1]
    states = 2 * half_states
    lanes = first.shape[1]
    core = lax.axis_index("mpo")
    totals = jnp.sum(gathered[...], axis=0)
    lane = lax.broadcasted_iota(jnp.int32, totals.shape, 1)
    s_aa, s_ay, s_yy, s_az, s_yz = (
        jnp.sum(jnp.where(lane == i, totals, 0.0), axis=1, keepdims=True) for i in range(5)
    )
    scale_sq = s_aa / entries + EPSILON
    shrunk = s_ay / entries / scale_sq
    residual_sq = jnp.maximum(s_yy - 2.0 * shrunk * s_ay + shrunk * shrunk * s_aa, 0.0)
    residual_norm = jnp.sqrt(residual_sq / scale_sq / entries * (GROW * GROW) + EPSILON)
    factor = GROW / (jnp.sqrt(scale_sq) * residual_norm)
    final = (s_yz - shrunk * s_yy - shrunk * s_az + shrunk * shrunk * s_ay) / entries
    gamma = final * factor * factor * GROW
    r = lax.broadcasted_iota(jnp.int32, projected.shape, 0)
    c = lax.broadcasted_iota(jnp.int32, projected.shape, 1)
    diagonal = jnp.where(r == 0, shrunk * GROW, gamma)
    projected[...] = jnp.where(r == c, diagonal, residual_norm)

    size = half * half_states
    own = state_half(vector[...].astype(jnp.float32), states, core).reshape(2 * size, lanes)
    ours = jnp.where(core == 0, own[:size, :], own[size:, :])
    theirs = jnp.where(core == 0, own[size:, :], own[:size, :])
    mine = [state_half(image[...], states, core) for image in (first, second)]
    for index, (y, z), a in (
        (core, mine, ours),
        (1 - core, (got[0:half], got[half : 2 * half]), theirs),
    ):
        y = y.reshape(size, lanes)
        z = z.reshape(size, lanes)
        place = pl.ds(pl.multiple_of(index * size, size), size)
        basis_two[place, :] = ((y - shrunk * a) * factor).astype(jnp.bfloat16)
        image_two[place, :] = ((z - shrunk * y) * (factor * GROW)).astype(jnp.bfloat16)


def call(kernel, operands, outs, scratch, name, cost=None):
    return pl.pallas_call(
        kernel,
        out_shape=tuple(jax.ShapeDtypeStruct(shape, dtype) for shape, dtype in outs),
        in_specs=[WHOLE] * len(operands),
        out_specs=(WHOLE,) * len(outs),
        scratch_shapes=[pltpu.VMEM(shape, dtype) for shape, dtype in scratch],
        cost_estimate=cost,
        compiler_params=pltpu.CompilerParams(vmem_limit_bytes=VMEM_LIMIT),
        name=name,
    )(*operands)


def per_device(amplitudes, left_env, right_env, mpo_left, mpo_right, sector_table):
    rows, states, columns = amplitudes.shape
    band = left_env.shape[2]
    bonds = mpo_left.shape[0]
    half = rows // 2
    half_states = states // 2
    size = half * states
    block = lax.axis_index("brow")
    core = lax.axis_index("mpo")
    axes = ("brow", "bcol", "mpo")
    peers = lax.axis_size(axes)
    entries = float(rows * lax.axis_size("brow") * states * columns * lax.axis_size("bcol"))
    f32, bf16 = jnp.float32, jnp.bfloat16
    flat = amplitudes.reshape(rows * states, columns)

    env_there = swap_cores(left_env)
    direct_one = trade(flat, (False, True))

    outside = jnp.full((rows,), -1, dtype=jnp.int32)
    padded = jnp.concatenate([outside, sector_table, outside])
    own_labels = lax.dynamic_slice_in_dim(padded, (block + 1) * rows + core * half, half, 0)
    partner = lax.dynamic_slice_in_dim(padded, block * rows, 3 * rows, 0)
    mask = (own_labels[:, None] == partner[None, :]).astype(f32)
    both = jnp.concatenate([mpo_left, mpo_right], axis=0)
    both = jnp.transpose(both, (0, 2, 3, 1)).reshape(2 * bonds * states, bonds)
    env, coupling = call(
        prepare_kernel,
        (left_env, env_there, mask, both),
        (
            ((half * SLOT, band), bf16),
            ((bonds * states, states * SLOT), bf16),
        ),
        (
            ((-(-band // 128) * SLOT * half, 128), f32),
            ((SLOT * states, 128), f32),
            ((SLOT * states, 128), f32),
            ((states * SLOT, 128), f32),
            ((states * SLOT, SLOT), f32),
            ((states // LOCAL * SLOT * states, 128), f32),
        ),
        "operands",
        cost=pl.CostEstimate(flops=4 * 10**9, bytes_accessed=2**23, transcendentals=0),
    )
    direct_one, env, coupling = lax.optimization_barrier((direct_one, env, coupling))
    passed_one = swap_cores(direct_one)
    right = right_env.reshape(bonds * columns, columns)

    work = (
        ((3 * rows, states * columns), bf16),
        ((half // GROUP, states * SLOT, GROUP * columns), bf16),
        ((size, bonds * columns), bf16),
    )
    laid = ((rows, states * columns), bf16)
    wide = ((rows * states, columns), f32)
    vector_rows, direct_rows = call(
        lay_kernel, (flat, direct_one), (laid, laid), (wide,), "rows", cost=SHORT
    )
    first, first_rows = call(
        first_kernel,
        (env, coupling, right, vector_rows, direct_rows, passed_one),
        (((size, columns), f32), ((half, states * columns), bf16)),
        (wide,) + work,
        "first_image",
    )
    (sums,) = call(sums_kernel, (first, flat), (((8, columns), f32),), (), "sums", cost=SHORT)

    even_rows = trade(first_rows, (False, False))
    odd_rows = trade(first_rows, (True, True))
    pieces = [(x, swap_cores(x)) for x in (first_rows, even_rows, odd_rows)]
    pieces = [x for pair in pieces for x in pair]

    second, sent, totals = call(
        second_kernel,
        (env, coupling, right, *pieces, first, flat, sums),
        (
            ((size, columns), f32),
            ((2 * half, half_states, columns), f32),
            ((peers, 1, columns), f32),
        ),
        work,
        "second_image",
    )
    got = swap_cores(sent)
    gathered = lax.all_to_all(totals, axes, 0, 0)

    def finish(*refs):
        final_kernel(entries, *refs)

    image_two, basis_two, projected = call(
        finish,
        (first, second, got, flat, gathered),
        (
            ((rows * half_states, columns), bf16),
            ((rows * half_states, columns), bf16),
            ((2, 2), f32),
        ),
        (),
        "outputs",
    )
    shape = (rows, half_states, columns)
    return (image_two.reshape(shape), basis_two.reshape(shape), projected)


def solution(mesh):
    return jax.shard_map(
        per_device,
        mesh=mesh,
        in_specs=(
            P(("groups", "brow"), None, "bcol"),
            P(("groups", "mpo"), "brow", None),
            P("groups", "bcol", None),
            P(),
            P(),
            P("groups"),
        ),
        out_specs=(
            P(("groups", "brow"), "mpo", "bcol"),
            P(("groups", "brow"), "mpo", "bcol"),
            P("groups", None),
        ),
        check_vma=False,
    )
```

```python
import jax
import jax.numpy as jnp
from jax import lax
from jax.experimental import pallas as pl
from jax.experimental.pallas import tpu as pltpu
from jax.sharding import PartitionSpec as P

EPSILON = 1e-06
SHRINK = 2.0**-12
GROW = 1.0 / SHRINK
SLOT = 32
LOCAL = 4
GROUP = 16
VMEM_LIMIT = 40 * 2**20
SHORT = pl.CostEstimate(flops=10**9, bytes_accessed=2**21, transcendentals=0)
WHOLE = pl.BlockSpec(memory_space=pltpu.VMEM)


def swap_cores(x):
    return lax.ppermute(x, "mpo", [(0, 1), (1, 0)])


def partner_of(block, slab, odd):
    blocks, slabs = lax.axis_size("brow"), lax.axis_size("bcol")
    other = (block + 1 if block % 2 else block - 1) if odd else block ^ 1
    if 0 <= other < blocks:
        return other, slab
    return block, slab ^ 1 if slab ^ 1 < slabs else slab


def place_of(block, slab, core):
    return (block * lax.axis_size("bcol") + slab) * 2 + core


def trade(x, odd):
    pairs = []
    for block in range(lax.axis_size("brow")):
        for slab in range(lax.axis_size("bcol")):
            for core in range(2):
                other = partner_of(block, slab, odd[core])
                pairs.append((place_of(block, slab, core), place_of(*other, core)))
    return lax.ppermute(x, ("brow", "bcol", "mpo"), pairs)


def halo_places(rows):
    even = lax.rem(lax.axis_index("brow") + lax.axis_index("mpo"), 2) == 0
    direct = jnp.where(even, 2 * rows, 0)
    return pl.multiple_of(direct, rows), pl.multiple_of(2 * rows - direct, rows)


def states_apart(wide, rows, states, store):
    lanes = wide.shape[1]
    for state in range(states):
        piece = wide[pl.ds(state, rows, stride=states), :].astype(jnp.bfloat16)
        store(slice(state * lanes, (state + 1) * lanes), piece)


def prepare_kernel(
    env_mine, env_there, mask, both_mpo,
    env, coupling,
    by_bond, left_pad, right_pad, left_rows, right_rows, spread,
):
    core = lax.axis_index("mpo")
    share, rows, _ = env_mine.shape
    half = rows // 2
    here = pl.ds(pl.multiple_of(core * half, half), half)
    part = SLOT // 2
    used, bonds = both_mpo.shape[0] // 2, both_mpo.shape[1]
    states = used // bonds
    left_pad[...] = jnp.zeros_like(left_pad)
    right_pad[...] = jnp.zeros_like(right_pad)
    left_pad[0:used, 0:bonds] = both_mpo[0:used, :]
    right_pad[0:used, 0:bonds] = both_mpo[used : 2 * used, :]
    for state in range(states):
        for group, owner in enumerate((core, 1 - core)):
            start = state * SLOT + group * part
            left_rows[start : start + part, :] = left_pad[
                pl.ds(owner * (share * states) + state, part, stride=states), :
            ]
        across = right_pad[pl.ds(state, SLOT, stride=states), :]
        right_rows[state * SLOT : (state + 1) * SLOT, :] = jnp.transpose(across)[0:SLOT, :]
    joined = lax.dot_general(
        right_rows[...],
        left_rows[:, 0:SLOT],
        (((1,), (1,)), ((), ())),
        precision=lax.Precision.HIGHEST,
        preferred_element_type=jnp.float32,
    )
    width = LOCAL * SLOT
    for i in range(LOCAL):
        for j in range(LOCAL):
            for inner in range(LOCAL):
                start = inner * SLOT * states + i * LOCAL + j
                spread[pl.ds(start, SLOT, stride=states), :] = joined[
                    (j * LOCAL + inner) * SLOT : (j * LOCAL + inner + 1) * SLOT,
                    i * width : (i + 1) * width,
                ]
    for inner in range(LOCAL):
        start = inner * SLOT * states
        coupling[:, inner * width : (inner + 1) * width] = spread[
            start : start + used, :
        ].astype(jnp.bfloat16)

    band = mask.shape[1]
    by_bond[...] = jnp.zeros_like(by_bond)
    for low in range(0, band, 128):
        width = min(128, band - low)
        base = low // 128 * SLOT * half
        for group, source in enumerate((env_mine, env_there)):
            for bond in range(share):
                start = base + (group * part + bond) * half
                piece = source[bond, here, low : low + width].astype(jnp.float32)
                by_bond[start : start + half, 0:width] = piece
        for row in range(half):
            piece = by_bond[pl.ds(base + row, SLOT, stride=half), :][:, 0:width]
            kept = jnp.where(mask[row : row + 1, low : low + width] > 0.0, piece, 0.0)
            env[row * SLOT : (row + 1) * SLOT, low : low + width] = kept.astype(jnp.bfloat16)


def apply_steps(env, coupling, right, extended, contracted, mixed, image):
    groups, depth, width = contracted.shape
    lanes = right.shape[1]
    group = width // lanes
    states = depth // SLOT
    bonds = mixed.shape[1] // lanes
    product = jnp.dot(env[...], extended[...], preferred_element_type=jnp.float32)
    product = product.astype(jnp.bfloat16)
    for state in range(states):
        place = state % LOCAL * LOCAL + state // LOCAL
        for row in range(groups * group):
            contracted[
                row // group,
                place * SLOT : (place + 1) * SLOT,
                row % group * lanes : (row % group + 1) * lanes,
            ] = product[row * SLOT : (row + 1) * SLOT, state * lanes : (state + 1) * lanes]

    def mix(step):
        product = jnp.dot(coupling[...], contracted[step], preferred_element_type=jnp.float32)
        product = product.astype(jnp.bfloat16)
        for part in range(group):
            start = (group * step + part) * states
            for bond in range(bonds):
                mixed[start : start + states, bond * lanes : (bond + 1) * lanes] = product[
                    bond * states : (bond + 1) * states, part * lanes : (part + 1) * lanes
                ]

    def finish(step):
        place = slice(group * step * states, group * (step + 1) * states)
        image[place, :] = SHRINK * jnp.dot(
            mixed[place, :], right[...], preferred_element_type=jnp.float32
        )

    mix(0)
    for step in range(groups):
        if step + 1 < groups:
            mix(step + 1)
        finish(step)


def column_sum(x):
    return jnp.sum(x, axis=0, keepdims=True)


def state_half(image, states, index):
    pieces = image.reshape(image.shape[0] // states, states, image.shape[1])
    return jnp.where(index == 0, pieces[:, : states // 2, :], pieces[:, states // 2 :, :])


def lay_kernel(vector, direct, vector_rows, direct_rows, wide):
    rows, width = vector_rows.shape
    states = width // vector.shape[1]
    for source, target in ((vector, vector_rows), (direct, direct_rows)):
        wide[...] = source[...].astype(jnp.float32)

        def store(columns, piece, target=target):
            target[:, columns] = piece

        states_apart(wide, rows, states, store)


def first_kernel(
    env, coupling, right, vector_rows, direct_rows, passed_in,
    image, image_rows,
    wide, extended, contracted, mixed,
):
    rows = vector_rows.shape[0]
    states = passed_in.shape[0] // rows
    half = image.shape[0]
    direct, passed = halo_places(rows)
    extended[rows : 2 * rows, :] = vector_rows[...]
    extended[pl.ds(direct, rows), :] = direct_rows[...]
    wide[...] = passed_in[...].astype(jnp.float32)

    def store(columns, piece):
        extended[pl.ds(passed, rows), columns] = piece

    states_apart(wide, rows, states, store)
    apply_steps(env, coupling, right, extended, contracted, mixed, image)

    def store_rows(columns, piece):
        image_rows[:, columns] = piece

    states_apart(image, half // states, states, store_rows)


def sums_kernel(image, vector, sums):
    half, lanes = image.shape
    start = pl.multiple_of(lax.axis_index("mpo") * half, half)
    own = vector[pl.ds(start, half), :].astype(jnp.float32)
    out = image[...]
    sums[...] = jnp.concatenate(
        [column_sum(own * own), column_sum(own * out), column_sum(out * out)]
        + [jnp.zeros((5, lanes), jnp.float32)],
        axis=0,
    )


def second_kernel(
    env, coupling, right, own_here, own_there, even_here, even_there, odd_here, odd_there,
    first, vector, sums,
    image, sent, totals,
    extended, contracted, mixed,
):
    part = own_here.shape[0]
    rows = 2 * part
    half = first.shape[0]
    core = lax.axis_index("mpo")
    even = lax.rem(lax.axis_index("brow"), 2) == 0
    above, below = jnp.where(even, 2 * rows, 0), jnp.where(even, 0, 2 * rows)
    for base, here, there in (
        (rows, own_here, own_there), (above, even_here, even_there), (below, odd_here, odd_there)
    ):
        extended[pl.ds(pl.multiple_of(base + core * part, part), part), :] = here[...]
        extended[pl.ds(pl.multiple_of(base + (1 - core) * part, part), part), :] = there[...]
    apply_steps(env, coupling, right, extended, contracted, mixed, image)
    out = image[...]
    states = half // part
    sent[0:part] = state_half(first[...], states, 1 - core)
    sent[part : 2 * part] = state_half(out, states, 1 - core)
    own = vector[pl.ds(pl.multiple_of(core * half, half), half), :].astype(jnp.float32)
    lanes = out.shape[1]
    columns = jnp.concatenate(
        [sums[0:3, :], column_sum(own * out), column_sum(first[...] * out)]
        + [jnp.zeros((3, lanes), jnp.float32)],
        axis=0,
    )
    lane = lax.broadcasted_iota(jnp.int32, columns.shape, 1)
    row = lax.broadcasted_iota(jnp.int32, columns.shape, 0)
    spread = jnp.where(lane == row, jnp.sum(columns, axis=1, keepdims=True), 0.0)
    totals[...] = jnp.broadcast_to(column_sum(spread)[None], totals.shape)


def final_kernel(
    entries, first, second, got, vector, gathered,
    image_two, basis_two, projected,
):
    half = got.shape[0] // 2
    half_states = got.shape[1]
    states = 2 * half_states
    lanes = first.shape[1]
    core = lax.axis_index("mpo")
    totals = jnp.sum(gathered[...], axis=0)
    lane = lax.broadcasted_iota(jnp.int32, totals.shape, 1)
    s_aa, s_ay, s_yy, s_az, s_yz = (
        jnp.sum(jnp.where(lane == i, totals, 0.0), axis=1, keepdims=True) for i in range(5)
    )
    scale_sq = s_aa / entries + EPSILON
    shrunk = s_ay / entries / scale_sq
    residual_sq = jnp.maximum(s_yy - 2.0 * shrunk * s_ay + shrunk * shrunk * s_aa, 0.0)
    residual_norm = jnp.sqrt(residual_sq / scale_sq / entries * (GROW * GROW) + EPSILON)
    factor = GROW / (jnp.sqrt(scale_sq) * residual_norm)
    final = (s_yz - shrunk * s_yy - shrunk * s_az + shrunk * shrunk * s_ay) / entries
    gamma = final * factor * factor * GROW
    r = lax.broadcasted_iota(jnp.int32, projected.shape, 0)
    c = lax.broadcasted_iota(jnp.int32, projected.shape, 1)
    diagonal = jnp.where(r == 0, shrunk * GROW, gamma)
    projected[...] = jnp.where(r == c, diagonal, residual_norm)

    size = half * half_states
    own = state_half(vector[...].astype(jnp.float32), states, core).reshape(2 * size, lanes)
    ours = jnp.where(core == 0, own[:size, :], own[size:, :])
    theirs = jnp.where(core == 0, own[size:, :], own[:size, :])
    mine = [state_half(image[...], states, core) for image in (first, second)]
    for index, (y, z), a in (
        (core, mine, ours),
        (1 - core, (got[0:half], got[half : 2 * half]), theirs),
    ):
        y = y.reshape(size, lanes)
        z = z.reshape(size, lanes)
        place = pl.ds(pl.multiple_of(index * size, size), size)
        basis_two[place, :] = ((y - shrunk * a) * factor).astype(jnp.bfloat16)
        image_two[place, :] = ((z - shrunk * y) * (factor * GROW)).astype(jnp.bfloat16)


def call(kernel, operands, outs, scratch, name, cost=None):
    return pl.pallas_call(
        kernel,
        out_shape=tuple(jax.ShapeDtypeStruct(shape, dtype) for shape, dtype in outs),
        in_specs=[WHOLE] * len(operands),
        out_specs=(WHOLE,) * len(outs),
        scratch_shapes=[pltpu.VMEM(shape, dtype) for shape, dtype in scratch],
        cost_estimate=cost,
        compiler_params=pltpu.CompilerParams(vmem_limit_bytes=VMEM_LIMIT),
        name=name,
    )(*operands)


def per_device(amplitudes, left_env, right_env, mpo_left, mpo_right, sector_table):
    rows, states, columns = amplitudes.shape
    band = left_env.shape[2]
    bonds = mpo_left.shape[0]
    half = rows // 2
    half_states = states // 2
    size = half * states
    block = lax.axis_index("brow")
    core = lax.axis_index("mpo")
    axes = ("brow", "bcol", "mpo")
    peers = lax.axis_size(axes)
    entries = float(rows * lax.axis_size("brow") * states * columns * lax.axis_size("bcol"))
    f32, bf16 = jnp.float32, jnp.bfloat16
    flat = amplitudes.reshape(rows * states, columns)

    env_there = swap_cores(left_env)
    direct_one = trade(flat, (False, True))

    outside = jnp.full((rows,), -1, dtype=jnp.int32)
    padded = jnp.concatenate([outside, sector_table, outside])
    own_labels = lax.dynamic_slice_in_dim(padded, (block + 1) * rows + core * half, half, 0)
    partner = lax.dynamic_slice_in_dim(padded, block * rows, 3 * rows, 0)
    mask = (own_labels[:, None] == partner[None, :]).astype(f32)
    both = jnp.concatenate([mpo_left, mpo_right], axis=0)
    both = jnp.transpose(both, (0, 2, 3, 1)).reshape(2 * bonds * states, bonds)
    env, coupling = call(
        prepare_kernel,
        (left_env, env_there, mask, both),
        (
            ((half * SLOT, band), bf16),
            ((bonds * states, states * SLOT), bf16),
        ),
        (
            ((-(-band // 128) * SLOT * half, 128), f32),
            ((SLOT * states, 128), f32),
            ((SLOT * states, 128), f32),
            ((states * SLOT, 128), f32),
            ((states * SLOT, SLOT), f32),
            ((states // LOCAL * SLOT * states, 128), f32),
        ),
        "operands",
        cost=pl.CostEstimate(flops=4 * 10**9, bytes_accessed=2**23, transcendentals=0),
    )
    direct_one, env, coupling = lax.optimization_barrier((direct_one, env, coupling))
    passed_one = swap_cores(direct_one)
    right = right_env.reshape(bonds * columns, columns)

    work = (
        ((3 * rows, states * columns), bf16),
        ((half // GROUP, states * SLOT, GROUP * columns), bf16),
        ((size, bonds * columns), bf16),
    )
    laid = ((rows, states * columns), bf16)
    wide = ((rows * states, columns), f32)
    vector_rows, direct_rows = call(
        lay_kernel, (flat, direct_one), (laid, laid), (wide,), "rows", cost=SHORT
    )
    first, first_rows = call(
        first_kernel,
        (env, coupling, right, vector_rows, direct_rows, passed_one),
        (((size, columns), f32), ((half, states * columns), bf16)),
        (wide,) + work,
        "first_image",
    )
    (sums,) = call(sums_kernel, (first, flat), (((8, columns), f32),), (), "sums", cost=SHORT)

    even_rows = trade(first_rows, (False, False))
    odd_rows = trade(first_rows, (True, True))
    pieces = [(x, swap_cores(x)) for x in (first_rows, even_rows, odd_rows)]
    pieces = [x for pair in pieces for x in pair]

    second, sent, totals = call(
        second_kernel,
        (env, coupling, right, *pieces, first, flat, sums),
        (
            ((size, columns), f32),
            ((2 * half, half_states, columns), f32),
            ((peers, 1, columns), f32),
        ),
        work,
        "second_image",
    )
    got = swap_cores(sent)
    gathered = lax.all_to_all(totals, axes, 0, 0)

    def finish(*refs):
        final_kernel(entries, *refs)

    image_two, basis_two, projected = call(
        finish,
        (first, second, got, flat, gathered),
        (
            ((rows * half_states, columns), bf16),
            ((rows * half_states, columns), bf16),
            ((2, 2), f32),
        ),
        (),
        "outputs",
    )
    shape = (rows, half_states, columns)
    return (image_two.reshape(shape), basis_two.reshape(shape), projected)


def solution(mesh):
    return jax.shard_map(
        per_device,
        mesh=mesh,
        in_specs=(
            P(("groups", "brow"), None, "bcol"),
            P(("groups", "mpo"), "brow", None),
            P("groups", "bcol", None),
            P(),
            P(),
            P("groups"),
        ),
        out_specs=(
            P(("groups", "brow"), "mpo", "bcol"),
            P(("groups", "brow"), "mpo", "bcol"),
            P("groups", None),
        ),
        check_vma=False,
    )
```

```python
import jax
import jax.numpy as jnp
from jax import lax
from jax.experimental import pallas as pl
from jax.experimental.pallas import tpu as pltpu
from jax.sharding import PartitionSpec as P

EPSILON = 1e-06
SHRINK = 2.0**-12
GROW = 1.0 / SHRINK
SLOT = 32
LOCAL = 4
GROUP = 8
VMEM_LIMIT = 40 * 2**20
SHORT = pl.CostEstimate(flops=10**9, bytes_accessed=2**21, transcendentals=0)
WHOLE = pl.BlockSpec(memory_space=pltpu.VMEM)


def swap_cores(x):
    return lax.ppermute(x, "mpo", [(0, 1), (1, 0)])


def partner_of(block, slab, odd):
    blocks, slabs = lax.axis_size("brow"), lax.axis_size("bcol")
    other = (block + 1 if block % 2 else block - 1) if odd else block ^ 1
    if 0 <= other < blocks:
        return other, slab
    return block, slab ^ 1 if slab ^ 1 < slabs else slab


def place_of(block, slab, core):
    return (block * lax.axis_size("bcol") + slab) * 2 + core


def trade(x, odd):
    pairs = []
    for block in range(lax.axis_size("brow")):
        for slab in range(lax.axis_size("bcol")):
            for core in range(2):
                other = partner_of(block, slab, odd[core])
                pairs.append((place_of(block, slab, core), place_of(*other, core)))
    return lax.ppermute(x, ("brow", "bcol", "mpo"), pairs)


def halo_places(rows):
    even = lax.rem(lax.axis_index("brow") + lax.axis_index("mpo"), 2) == 0
    direct = jnp.where(even, 2 * rows, 0)
    return pl.multiple_of(direct, rows), pl.multiple_of(2 * rows - direct, rows)


def states_apart(wide, rows, states, store):
    lanes = wide.shape[1]
    for state in range(states):
        piece = wide[pl.ds(state, rows, stride=states), :].astype(jnp.bfloat16)
        store(slice(state * lanes, (state + 1) * lanes), piece)


def prepare_kernel(
    env_mine, env_there, mask, both_mpo,
    env_one, env_two, coupling,
    env, by_bond, left_pad, right_pad, left_rows, right_rows, spread,
):
    core = lax.axis_index("mpo")
    share, rows, _ = env_mine.shape
    half = rows // 2
    here = pl.ds(pl.multiple_of(core * half, half), half)
    part = SLOT // 2
    used, bonds = both_mpo.shape[0] // 2, both_mpo.shape[1]
    states = used // bonds
    left_pad[...] = jnp.zeros_like(left_pad)
    right_pad[...] = jnp.zeros_like(right_pad)
    left_pad[0:used, 0:bonds] = both_mpo[0:used, :]
    right_pad[0:used, 0:bonds] = both_mpo[used : 2 * used, :]
    for state in range(states):
        for group, owner in enumerate((core, 1 - core)):
            start = state * SLOT + group * part
            left_rows[start : start + part, :] = left_pad[
                pl.ds(owner * (share * states) + state, part, stride=states), :
            ]
        across = right_pad[pl.ds(state, SLOT, stride=states), :]
        right_rows[state * SLOT : (state + 1) * SLOT, :] = jnp.transpose(across)[0:SLOT, :]
    joined = lax.dot_general(
        right_rows[...],
        left_rows[:, 0:SLOT],
        (((1,), (1,)), ((), ())),
        precision=lax.Precision.HIGHEST,
        preferred_element_type=jnp.float32,
    )
    width = LOCAL * SLOT
    for i in range(LOCAL):
        for j in range(LOCAL):
            for inner in range(LOCAL):
                start = inner * SLOT * states + i * LOCAL + j
                spread[pl.ds(start, SLOT, stride=states), :] = joined[
                    (j * LOCAL + inner) * SLOT : (j * LOCAL + inner + 1) * SLOT,
                    i * width : (i + 1) * width,
                ]
    for inner in range(LOCAL):
        start = inner * SLOT * states
        coupling[:, inner * width : (inner + 1) * width] = spread[
            start : start + used, :
        ].astype(jnp.bfloat16)

    band = mask.shape[1]
    by_bond[...] = jnp.zeros_like(by_bond)
    for low in range(0, band, 128):
        width = min(128, band - low)
        base = low // 128 * SLOT * half
        for group, source in enumerate((env_mine, env_there)):
            for bond in range(share):
                start = base + (group * part + bond) * half
                piece = source[bond, here, low : low + width].astype(jnp.float32)
                by_bond[start : start + half, 0:width] = piece
        for row in range(half):
            piece = by_bond[pl.ds(base + row, SLOT, stride=half), :][:, 0:width]
            kept = jnp.where(mask[row : row + 1, low : low + width] > 0.0, piece, 0.0)
            env[row * SLOT : (row + 1) * SLOT, low : low + width] = kept.astype(jnp.bfloat16)

    direct, passed = halo_places(rows)
    even = lax.rem(lax.axis_index("brow"), 2) == 0
    above, below = jnp.where(even, 2 * rows, 0), jnp.where(even, 0, 2 * rows)
    shares = [base + share * half for base in (rows, above, below) for share in (core, 1 - core)]
    for target, starts in ((env_one, (rows, direct, passed)), (env_two, shares)):
        size = band // len(starts)
        taken = lax.broadcasted_iota(jnp.int32, (band, band), 0)
        place = lax.broadcasted_iota(jnp.int32, (band, band), 1)
        chosen = jnp.zeros((band, band), jnp.bool_)
        for index, start in enumerate(starts):
            inside = (place >= index * size) & (place < (index + 1) * size)
            chosen = chosen | (inside & (taken == place + (start - index * size)))
        order = jnp.where(chosen, 1.0, 0.0).astype(jnp.bfloat16)
        moved = jnp.dot(env[...], order, preferred_element_type=jnp.float32)
        target[...] = moved.astype(jnp.bfloat16)


def apply_steps(env, coupling, right, pieces, contracted, mixed, image):
    groups, depth, width = contracted.shape
    lanes = right.shape[1]
    group = width // lanes
    states = depth // SLOT
    bonds = mixed.shape[1] // lanes
    extended = jnp.concatenate([piece[...] for piece in pieces], axis=0)
    product = jnp.dot(env[...], extended, preferred_element_type=jnp.float32)
    product = product.astype(jnp.bfloat16)
    for state in range(states):
        place = state % LOCAL * LOCAL + state // LOCAL
        for row in range(groups * group):
            contracted[
                row // group,
                place * SLOT : (place + 1) * SLOT,
                row % group * lanes : (row % group + 1) * lanes,
            ] = product[row * SLOT : (row + 1) * SLOT, state * lanes : (state + 1) * lanes]

    def mix(step):
        product = jnp.dot(coupling[...], contracted[step], preferred_element_type=jnp.float32)
        product = product.astype(jnp.bfloat16)
        for part in range(group):
            start = (group * step + part) * states
            for bond in range(bonds):
                mixed[start : start + states, bond * lanes : (bond + 1) * lanes] = product[
                    bond * states : (bond + 1) * states, part * lanes : (part + 1) * lanes
                ]

    def finish(step):
        place = slice(group * step * states, group * (step + 1) * states)
        image[place, :] = SHRINK * jnp.dot(
            mixed[place, :], right[...], preferred_element_type=jnp.float32
        )

    mix(0)
    for step in range(groups):
        if step + 1 < groups:
            mix(step + 1)
        finish(step)


def column_sum(x):
    return jnp.sum(x, axis=0, keepdims=True)


def state_half(image, states, index):
    pieces = image.reshape(image.shape[0] // states, states, image.shape[1])
    return jnp.where(index == 0, pieces[:, : states // 2, :], pieces[:, states // 2 :, :])


def lay_kernel(vector, direct, vector_rows, direct_rows, wide):
    rows, width = vector_rows.shape
    states = width // vector.shape[1]
    for source, target in ((vector, vector_rows), (direct, direct_rows)):
        wide[...] = source[...].astype(jnp.float32)

        def store(columns, piece, target=target):
            target[:, columns] = piece

        states_apart(wide, rows, states, store)


def first_kernel(
    env, coupling, right, vector_rows, direct_rows, passed_in,
    image, image_rows,
    wide, passed_rows, contracted, mixed,
):
    rows = vector_rows.shape[0]
    states = passed_in.shape[0] // rows
    half = image.shape[0]
    wide[...] = passed_in[...].astype(jnp.float32)

    def store(columns, piece):
        passed_rows[:, columns] = piece

    states_apart(wide, rows, states, store)
    pieces = (vector_rows, direct_rows, passed_rows)
    apply_steps(env, coupling, right, pieces, contracted, mixed, image)

    def store_rows(columns, piece):
        image_rows[:, columns] = piece

    states_apart(image, half // states, states, store_rows)


def sums_kernel(image, vector, sums):
    half, lanes = image.shape
    start = pl.multiple_of(lax.axis_index("mpo") * half, half)
    own = vector[pl.ds(start, half), :].astype(jnp.float32)
    out = image[...]
    sums[...] = jnp.concatenate(
        [column_sum(own * own), column_sum(own * out), column_sum(out * out)]
        + [jnp.zeros((5, lanes), jnp.float32)],
        axis=0,
    )


def second_kernel(
    env, coupling, right, own_here, own_there, even_here, even_there, odd_here, odd_there,
    first, vector, sums,
    image, sent, totals,
    contracted, mixed,
):
    part = own_here.shape[0]
    half = first.shape[0]
    core = lax.axis_index("mpo")
    pieces = (own_here, own_there, even_here, even_there, odd_here, odd_there)
    apply_steps(env, coupling, right, pieces, contracted, mixed, image)
    out = image[...]
    states = half // part
    sent[0:part] = state_half(first[...], states, 1 - core)
    sent[part : 2 * part] = state_half(out, states, 1 - core)
    own = vector[pl.ds(pl.multiple_of(core * half, half), half), :].astype(jnp.float32)
    lanes = out.shape[1]
    columns = jnp.concatenate(
        [sums[0:3, :], column_sum(own * out), column_sum(first[...] * out)]
        + [jnp.zeros((3, lanes), jnp.float32)],
        axis=0,
    )
    lane = lax.broadcasted_iota(jnp.int32, columns.shape, 1)
    row = lax.broadcasted_iota(jnp.int32, columns.shape, 0)
    spread = jnp.where(lane == row, jnp.sum(columns, axis=1, keepdims=True), 0.0)
    totals[...] = jnp.broadcast_to(column_sum(spread)[None], totals.shape)


def final_kernel(
    entries, first, second, got, vector, gathered,
    image_two, basis_two, projected,
):
    half = got.shape[0] // 2
    half_states = got.shape[1]
    states = 2 * half_states
    lanes = first.shape[1]
    core = lax.axis_index("mpo")
    totals = jnp.sum(gathered[...], axis=0)
    lane = lax.broadcasted_iota(jnp.int32, totals.shape, 1)
    s_aa, s_ay, s_yy, s_az, s_yz = (
        jnp.sum(jnp.where(lane == i, totals, 0.0), axis=1, keepdims=True) for i in range(5)
    )
    scale_sq = s_aa / entries + EPSILON
    shrunk = s_ay / entries / scale_sq
    residual_sq = jnp.maximum(s_yy - 2.0 * shrunk * s_ay + shrunk * shrunk * s_aa, 0.0)
    residual_norm = jnp.sqrt(residual_sq / scale_sq / entries * (GROW * GROW) + EPSILON)
    factor = GROW / (jnp.sqrt(scale_sq) * residual_norm)
    final = (s_yz - shrunk * s_yy - shrunk * s_az + shrunk * shrunk * s_ay) / entries
    gamma = final * factor * factor * GROW
    r = lax.broadcasted_iota(jnp.int32, projected.shape, 0)
    c = lax.broadcasted_iota(jnp.int32, projected.shape, 1)
    diagonal = jnp.where(r == 0, shrunk * GROW, gamma)
    projected[...] = jnp.where(r == c, diagonal, residual_norm)

    size = half * half_states
    own = state_half(vector[...].astype(jnp.float32), states, core).reshape(2 * size, lanes)
    ours = jnp.where(core == 0, own[:size, :], own[size:, :])
    theirs = jnp.where(core == 0, own[size:, :], own[:size, :])
    mine = [state_half(image[...], states, core) for image in (first, second)]
    for index, (y, z), a in (
        (core, mine, ours),
        (1 - core, (got[0:half], got[half : 2 * half]), theirs),
    ):
        y = y.reshape(size, lanes)
        z = z.reshape(size, lanes)
        place = pl.ds(pl.multiple_of(index * size, size), size)
        basis_two[place, :] = ((y - shrunk * a) * factor).astype(jnp.bfloat16)
        image_two[place, :] = ((z - shrunk * y) * (factor * GROW)).astype(jnp.bfloat16)


def call(kernel, operands, outs, scratch, name, cost=None):
    return pl.pallas_call(
        kernel,
        out_shape=tuple(jax.ShapeDtypeStruct(shape, dtype) for shape, dtype in outs),
        in_specs=[WHOLE] * len(operands),
        out_specs=(WHOLE,) * len(outs),
        scratch_shapes=[pltpu.VMEM(shape, dtype) for shape, dtype in scratch],
        cost_estimate=cost,
        compiler_params=pltpu.CompilerParams(vmem_limit_bytes=VMEM_LIMIT),
        name=name,
    )(*operands)


def per_device(amplitudes, left_env, right_env, mpo_left, mpo_right, sector_table):
    rows, states, columns = amplitudes.shape
    band = left_env.shape[2]
    bonds = mpo_left.shape[0]
    half = rows // 2
    half_states = states // 2
    size = half * states
    block = lax.axis_index("brow")
    core = lax.axis_index("mpo")
    axes = ("brow", "bcol", "mpo")
    peers = lax.axis_size(axes)
    entries = float(rows * lax.axis_size("brow") * states * columns * lax.axis_size("bcol"))
    f32, bf16 = jnp.float32, jnp.bfloat16
    flat = amplitudes.reshape(rows * states, columns)

    env_there = swap_cores(left_env)
    direct_one = trade(flat, (False, True))

    outside = jnp.full((rows,), -1, dtype=jnp.int32)
    padded = jnp.concatenate([outside, sector_table, outside])
    own_labels = lax.dynamic_slice_in_dim(padded, (block + 1) * rows + core * half, half, 0)
    partner = lax.dynamic_slice_in_dim(padded, block * rows, 3 * rows, 0)
    mask = (own_labels[:, None] == partner[None, :]).astype(f32)
    both = jnp.concatenate([mpo_left, mpo_right], axis=0)
    both = jnp.transpose(both, (0, 2, 3, 1)).reshape(2 * bonds * states, bonds)
    env_one, env_two, coupling = call(
        prepare_kernel,
        (left_env, env_there, mask, both),
        (
            ((half * SLOT, band), bf16),
            ((half * SLOT, band), bf16),
            ((bonds * states, states * SLOT), bf16),
        ),
        (
            ((half * SLOT, band), bf16),
            ((-(-band // 128) * SLOT * half, 128), f32),
            ((SLOT * states, 128), f32),
            ((SLOT * states, 128), f32),
            ((states * SLOT, 128), f32),
            ((states * SLOT, SLOT), f32),
            ((states // LOCAL * SLOT * states, 128), f32),
        ),
        "operands",
        cost=pl.CostEstimate(flops=4 * 10**9, bytes_accessed=2**23, transcendentals=0),
    )
    direct_one, env_one, coupling = lax.optimization_barrier((direct_one, env_one, coupling))
    passed_one = swap_cores(direct_one)
    right = right_env.reshape(bonds * columns, columns)

    work = (
        ((half // GROUP, states * SLOT, GROUP * columns), bf16),
        ((size, bonds * columns), bf16),
    )
    laid = ((rows, states * columns), bf16)
    wide = ((rows * states, columns), f32)
    vector_rows, direct_rows = call(
        lay_kernel, (flat, direct_one), (laid, laid), (wide,), "rows", cost=SHORT
    )
    first, first_rows = call(
        first_kernel,
        (env_one, coupling, right, vector_rows, direct_rows, passed_one),
        (((size, columns), f32), ((half, states * columns), bf16)),
        (wide, laid) + work,
        "first_image",
    )
    (sums,) = call(sums_kernel, (first, flat), (((8, columns), f32),), (), "sums", cost=SHORT)

    even_rows = trade(first_rows, (False, False))
    odd_rows = trade(first_rows, (True, True))
    pieces = [(x, swap_cores(x)) for x in (first_rows, even_rows, odd_rows)]
    pieces = [x for pair in pieces for x in pair]

    second, sent, totals = call(
        second_kernel,
        (env_two, coupling, right, *pieces, first, flat, sums),
        (
            ((size, columns), f32),
            ((2 * half, half_states, columns), f32),
            ((peers, 1, columns), f32),
        ),
        work,
        "second_image",
    )
    got = swap_cores(sent)
    gathered = lax.all_to_all(totals, axes, 0, 0)

    def finish(*refs):
        final_kernel(entries, *refs)

    image_two, basis_two, projected = call(
        finish,
        (first, second, got, flat, gathered),
        (
            ((rows * half_states, columns), bf16),
            ((rows * half_states, columns), bf16),
            ((2, 2), f32),
        ),
        (),
        "outputs",
    )
    shape = (rows, half_states, columns)
    return (image_two.reshape(shape), basis_two.reshape(shape), projected)


def solution(mesh):
    return jax.shard_map(
        per_device,
        mesh=mesh,
        in_specs=(
            P(("groups", "brow"), None, "bcol"),
            P(("groups", "mpo"), "brow", None),
            P("groups", "bcol", None),
            P(),
            P(),
            P("groups"),
        ),
        out_specs=(
            P(("groups", "brow"), "mpo", "bcol"),
            P(("groups", "brow"), "mpo", "bcol"),
            P("groups", None),
        ),
        check_vma=False,
    )
```

```python
import jax
import jax.numpy as jnp
from jax import lax
from jax.experimental import pallas as pl
from jax.experimental.pallas import tpu as pltpu
from jax.sharding import PartitionSpec as P

EPSILON = 1e-06
SHRINK = 2.0**-12
GROW = 1.0 / SHRINK
SLOT = 32
LOCAL = 4
GROUP = 16
VMEM_LIMIT = 40 * 2**20
SHORT = pl.CostEstimate(flops=10**9, bytes_accessed=2**21, transcendentals=0)
WHOLE = pl.BlockSpec(memory_space=pltpu.VMEM)


def swap_cores(x):
    return lax.ppermute(x, "mpo", [(0, 1), (1, 0)])


def partner_of(block, slab, odd):
    blocks, slabs = lax.axis_size("brow"), lax.axis_size("bcol")
    other = (block + 1 if block % 2 else block - 1) if odd else block ^ 1
    if 0 <= other < blocks:
        return other, slab
    return block, slab ^ 1 if slab ^ 1 < slabs else slab


def place_of(block, slab, core):
    return (block * lax.axis_size("bcol") + slab) * 2 + core


def trade(x, odd):
    pairs = []
    for block in range(lax.axis_size("brow")):
        for slab in range(lax.axis_size("bcol")):
            for core in range(2):
                other = partner_of(block, slab, odd[core])
                pairs.append((place_of(block, slab, core), place_of(*other, core)))
    return lax.ppermute(x, ("brow", "bcol", "mpo"), pairs)


def halo_places(rows):
    even = lax.rem(lax.axis_index("brow") + lax.axis_index("mpo"), 2) == 0
    direct = jnp.where(even, 2 * rows, 0)
    return pl.multiple_of(direct, rows), pl.multiple_of(2 * rows - direct, rows)


def states_apart(wide, rows, states, store):
    lanes = wide.shape[1]
    for state in range(states):
        piece = wide[pl.ds(state, rows, stride=states), :].astype(jnp.bfloat16)
        store(slice(state * lanes, (state + 1) * lanes), piece)


def prepare_kernel(
    env_mine, env_there, mask, both_mpo,
    env_one, env_two, coupling,
    env, by_bond, left_pad, right_pad, left_rows, right_rows, spread,
):
    core = lax.axis_index("mpo")
    share, rows, _ = env_mine.shape
    half = rows // 2
    here = pl.ds(pl.multiple_of(core * half, half), half)
    part = SLOT // 2
    used, bonds = both_mpo.shape[0] // 2, both_mpo.shape[1]
    states = used // bonds
    left_pad[...] = jnp.zeros_like(left_pad)
    right_pad[...] = jnp.zeros_like(right_pad)
    left_pad[0:used, 0:bonds] = both_mpo[0:used, :]
    right_pad[0:used, 0:bonds] = both_mpo[used : 2 * used, :]
    for state in range(states):
        for group, owner in enumerate((core, 1 - core)):
            start = state * SLOT + group * part
            left_rows[start : start + part, :] = left_pad[
                pl.ds(owner * (share * states) + state, part, stride=states), :
            ]
        across = right_pad[pl.ds(state, SLOT, stride=states), :]
        right_rows[state * SLOT : (state + 1) * SLOT, :] = jnp.transpose(across)[0:SLOT, :]
    joined = lax.dot_general(
        right_rows[...],
        left_rows[:, 0:SLOT],
        (((1,), (1,)), ((), ())),
        precision=lax.Precision.HIGHEST,
        preferred_element_type=jnp.float32,
    )
    width = LOCAL * SLOT
    for i in range(LOCAL):
        for j in range(LOCAL):
            for inner in range(LOCAL):
                start = inner * SLOT * states + i * LOCAL + j
                spread[pl.ds(start, SLOT, stride=states), :] = joined[
                    (j * LOCAL + inner) * SLOT : (j * LOCAL + inner + 1) * SLOT,
                    i * width : (i + 1) * width,
                ]
    for inner in range(LOCAL):
        start = inner * SLOT * states
        coupling[:, inner * width : (inner + 1) * width] = spread[
            start : start + used, :
        ].astype(jnp.bfloat16)

    band = mask.shape[1]
    by_bond[...] = jnp.zeros_like(by_bond)
    for low in range(0, band, 128):
        width = min(128, band - low)
        base = low // 128 * SLOT * half
        for group, source in enumerate((env_mine, env_there)):
            for bond in range(share):
                start = base + (group * part + bond) * half
                piece = source[bond, here, low : low + width].astype(jnp.float32)
                by_bond[start : start + half, 0:width] = piece
        for row in range(half):
            piece = by_bond[pl.ds(base + row, SLOT, stride=half), :][:, 0:width]
            kept = jnp.where(mask[row : row + 1, low : low + width] > 0.0, piece, 0.0)
            env[row * SLOT : (row + 1) * SLOT, low : low + width] = kept.astype(jnp.bfloat16)

    direct, passed = halo_places(rows)
    even = lax.rem(lax.axis_index("brow"), 2) == 0
    above, below = jnp.where(even, 2 * rows, 0), jnp.where(even, 0, 2 * rows)
    shares = [base + share * half for base in (rows, above, below) for share in (core, 1 - core)]
    for target, starts in ((env_one, (rows, direct, passed)), (env_two, shares)):
        size = band // len(starts)
        taken = lax.broadcasted_iota(jnp.int32, (band, band), 0)
        place = lax.broadcasted_iota(jnp.int32, (band, band), 1)
        chosen = jnp.zeros((band, band), jnp.bool_)
        for index, start in enumerate(starts):
            inside = (place >= index * size) & (place < (index + 1) * size)
            chosen = chosen | (inside & (taken == place + (start - index * size)))
        order = jnp.where(chosen, 1.0, 0.0).astype(jnp.bfloat16)
        moved = jnp.dot(env[...], order, preferred_element_type=jnp.float32)
        target[...] = moved.astype(jnp.bfloat16)


def apply_steps(env, coupling, right, pieces, contracted, mixed, image):
    groups, depth, width = contracted.shape
    lanes = right.shape[1]
    group = width // lanes
    states = depth // SLOT
    bonds = mixed.shape[1] // lanes
    extended = jnp.concatenate([piece[...] for piece in pieces], axis=0)
    product = jnp.dot(env[...], extended, preferred_element_type=jnp.float32)
    product = product.astype(jnp.bfloat16)
    for state in range(states):
        place = state % LOCAL * LOCAL + state // LOCAL
        for row in range(groups * group):
            contracted[
                row // group,
                place * SLOT : (place + 1) * SLOT,
                row % group * lanes : (row % group + 1) * lanes,
            ] = product[row * SLOT : (row + 1) * SLOT, state * lanes : (state + 1) * lanes]

    def mix(step):
        product = jnp.dot(coupling[...], contracted[step], preferred_element_type=jnp.float32)
        product = product.astype(jnp.bfloat16)
        for part in range(group):
            start = (group * step + part) * states
            for bond in range(bonds):
                mixed[start : start + states, bond * lanes : (bond + 1) * lanes] = product[
                    bond * states : (bond + 1) * states, part * lanes : (part + 1) * lanes
                ]

    def finish(step):
        place = slice(group * step * states, group * (step + 1) * states)
        image[place, :] = SHRINK * jnp.dot(
            mixed[place, :], right[...], preferred_element_type=jnp.float32
        )

    mix(0)
    for step in range(groups):
        if step + 1 < groups:
            mix(step + 1)
        finish(step)


def column_sum(x):
    return jnp.sum(x, axis=0, keepdims=True)


def state_half(image, states, index):
    pieces = image.reshape(image.shape[0] // states, states, image.shape[1])
    return jnp.where(index == 0, pieces[:, : states // 2, :], pieces[:, states // 2 :, :])


def lay_kernel(vector, direct, vector_rows, direct_rows, wide):
    rows, width = vector_rows.shape
    states = width // vector.shape[1]
    for source, target in ((vector, vector_rows), (direct, direct_rows)):
        wide[...] = source[...].astype(jnp.float32)

        def store(columns, piece, target=target):
            target[:, columns] = piece

        states_apart(wide, rows, states, store)


def first_kernel(
    env, coupling, right, vector_rows, direct_rows, passed_in,
    image, image_rows,
    wide, passed_rows, contracted, mixed,
):
    rows = vector_rows.shape[0]
    states = passed_in.shape[0] // rows
    half = image.shape[0]
    wide[...] = passed_in[...].astype(jnp.float32)

    def store(columns, piece):
        passed_rows[:, columns] = piece

    states_apart(wide, rows, states, store)
    pieces = (vector_rows, direct_rows, passed_rows)
    apply_steps(env, coupling, right, pieces, contracted, mixed, image)

    def store_rows(columns, piece):
        image_rows[:, columns] = piece

    states_apart(image, half // states, states, store_rows)


def sums_kernel(image, vector, sums):
    half, lanes = image.shape
    start = pl.multiple_of(lax.axis_index("mpo") * half, half)
    own = vector[pl.ds(start, half), :].astype(jnp.float32)
    out = image[...]
    sums[...] = jnp.concatenate(
        [column_sum(own * own), column_sum(own * out), column_sum(out * out)]
        + [jnp.zeros((5, lanes), jnp.float32)],
        axis=0,
    )


def second_kernel(
    env, coupling, right, own_here, own_there, even_here, even_there, odd_here, odd_there,
    first, vector, sums,
    image, sent, totals,
    contracted, mixed,
):
    part = own_here.shape[0]
    half = first.shape[0]
    core = lax.axis_index("mpo")
    pieces = (own_here, own_there, even_here, even_there, odd_here, odd_there)
    apply_steps(env, coupling, right, pieces, contracted, mixed, image)
    out = image[...]
    states = half // part
    sent[0:part] = state_half(first[...], states, 1 - core)
    sent[part : 2 * part] = state_half(out, states, 1 - core)
    own = vector[pl.ds(pl.multiple_of(core * half, half), half), :].astype(jnp.float32)
    lanes = out.shape[1]
    columns = jnp.concatenate(
        [sums[0:3, :], column_sum(own * out), column_sum(first[...] * out)]
        + [jnp.zeros((3, lanes), jnp.float32)],
        axis=0,
    )
    lane = lax.broadcasted_iota(jnp.int32, columns.shape, 1)
    row = lax.broadcasted_iota(jnp.int32, columns.shape, 0)
    spread = jnp.where(lane == row, jnp.sum(columns, axis=1, keepdims=True), 0.0)
    totals[...] = jnp.broadcast_to(column_sum(spread)[None], totals.shape)


def final_kernel(
    entries, first, second, got, vector, gathered,
    image_two, basis_two, projected,
):
    half = got.shape[0] // 2
    half_states = got.shape[1]
    states = 2 * half_states
    lanes = first.shape[1]
    core = lax.axis_index("mpo")
    totals = jnp.sum(gathered[...], axis=0)
    lane = lax.broadcasted_iota(jnp.int32, totals.shape, 1)
    s_aa, s_ay, s_yy, s_az, s_yz = (
        jnp.sum(jnp.where(lane == i, totals, 0.0), axis=1, keepdims=True) for i in range(5)
    )
    scale_sq = s_aa / entries + EPSILON
    shrunk = s_ay / entries / scale_sq
    residual_sq = jnp.maximum(s_yy - 2.0 * shrunk * s_ay + shrunk * shrunk * s_aa, 0.0)
    residual_norm = jnp.sqrt(residual_sq / scale_sq / entries * (GROW * GROW) + EPSILON)
    factor = GROW / (jnp.sqrt(scale_sq) * residual_norm)
    final = (s_yz - shrunk * s_yy - shrunk * s_az + shrunk * shrunk * s_ay) / entries
    gamma = final * factor * factor * GROW
    r = lax.broadcasted_iota(jnp.int32, projected.shape, 0)
    c = lax.broadcasted_iota(jnp.int32, projected.shape, 1)
    diagonal = jnp.where(r == 0, shrunk * GROW, gamma)
    projected[...] = jnp.where(r == c, diagonal, residual_norm)

    size = half * half_states
    own = state_half(vector[...].astype(jnp.float32), states, core).reshape(2 * size, lanes)
    ours = jnp.where(core == 0, own[:size, :], own[size:, :])
    theirs = jnp.where(core == 0, own[size:, :], own[:size, :])
    mine = [state_half(image[...], states, core) for image in (first, second)]
    for index, (y, z), a in (
        (core, mine, ours),
        (1 - core, (got[0:half], got[half : 2 * half]), theirs),
    ):
        y = y.reshape(size, lanes)
        z = z.reshape(size, lanes)
        place = pl.ds(pl.multiple_of(index * size, size), size)
        basis_two[place, :] = ((y - shrunk * a) * factor).astype(jnp.bfloat16)
        image_two[place, :] = ((z - shrunk * y) * (factor * GROW)).astype(jnp.bfloat16)


def call(kernel, operands, outs, scratch, name, cost=None):
    return pl.pallas_call(
        kernel,
        out_shape=tuple(jax.ShapeDtypeStruct(shape, dtype) for shape, dtype in outs),
        in_specs=[WHOLE] * len(operands),
        out_specs=(WHOLE,) * len(outs),
        scratch_shapes=[pltpu.VMEM(shape, dtype) for shape, dtype in scratch],
        cost_estimate=cost,
        compiler_params=pltpu.CompilerParams(vmem_limit_bytes=VMEM_LIMIT),
        name=name,
    )(*operands)


def per_device(amplitudes, left_env, right_env, mpo_left, mpo_right, sector_table):
    rows, states, columns = amplitudes.shape
    band = left_env.shape[2]
    bonds = mpo_left.shape[0]
    half = rows // 2
    half_states = states // 2
    size = half * states
    block = lax.axis_index("brow")
    core = lax.axis_index("mpo")
    axes = ("brow", "bcol", "mpo")
    peers = lax.axis_size(axes)
    entries = float(rows * lax.axis_size("brow") * states * columns * lax.axis_size("bcol"))
    f32, bf16 = jnp.float32, jnp.bfloat16
    flat = amplitudes.reshape(rows * states, columns)

    env_there = swap_cores(left_env)
    direct_one = trade(flat, (False, True))

    outside = jnp.full((rows,), -1, dtype=jnp.int32)
    padded = jnp.concatenate([outside, sector_table, outside])
    own_labels = lax.dynamic_slice_in_dim(padded, (block + 1) * rows + core * half, half, 0)
    partner = lax.dynamic_slice_in_dim(padded, block * rows, 3 * rows, 0)
    mask = (own_labels[:, None] == partner[None, :]).astype(f32)
    both = jnp.concatenate([mpo_left, mpo_right], axis=0)
    both = jnp.transpose(both, (0, 2, 3, 1)).reshape(2 * bonds * states, bonds)
    env_one, env_two, coupling = call(
        prepare_kernel,
        (left_env, env_there, mask, both),
        (
            ((half * SLOT, band), bf16),
            ((half * SLOT, band), bf16),
            ((bonds * states, states * SLOT), bf16),
        ),
        (
            ((half * SLOT, band), bf16),
            ((-(-band // 128) * SLOT * half, 128), f32),
            ((SLOT * states, 128), f32),
            ((SLOT * states, 128), f32),
            ((states * SLOT, 128), f32),
            ((states * SLOT, SLOT), f32),
            ((states // LOCAL * SLOT * states, 128), f32),
        ),
        "operands",
        cost=pl.CostEstimate(flops=4 * 10**9, bytes_accessed=2**23, transcendentals=0),
    )
    direct_one, env_one, coupling = lax.optimization_barrier((direct_one, env_one, coupling))
    passed_one = swap_cores(direct_one)
    right = right_env.reshape(bonds * columns, columns)

    work = (
        ((half // GROUP, states * SLOT, GROUP * columns), bf16),
        ((size, bonds * columns), bf16),
    )
    laid = ((rows, states * columns), bf16)
    wide = ((rows * states, columns), f32)
    vector_rows, direct_rows = call(
        lay_kernel, (flat, direct_one), (laid, laid), (wide,), "rows", cost=SHORT
    )
    first, first_rows = call(
        first_kernel,
        (env_one, coupling, right, vector_rows, direct_rows, passed_one),
        (((size, columns), f32), ((half, states * columns), bf16)),
        (wide, laid) + work,
        "first_image",
    )
    (sums,) = call(sums_kernel, (first, flat), (((8, columns), f32),), (), "sums", cost=SHORT)

    even_rows = trade(first_rows, (False, False))
    odd_rows = trade(first_rows, (True, True))
    pieces = [(x, swap_cores(x)) for x in (first_rows, even_rows, odd_rows)]
    pieces = [x for pair in pieces for x in pair]

    second, sent, totals = call(
        second_kernel,
        (env_two, coupling, right, *pieces, first, flat, sums),
        (
            ((size, columns), f32),
            ((2 * half, half_states, columns), f32),
            ((peers, 1, columns), f32),
        ),
        work,
        "second_image",
    )
    got = swap_cores(sent)
    gathered = lax.all_to_all(totals, axes, 0, 0)

    def finish(*refs):
        final_kernel(entries, *refs)

    image_two, basis_two, projected = call(
        finish,
        (first, second, got, flat, gathered),
        (
            ((rows * half_states, columns), bf16),
            ((rows * half_states, columns), bf16),
            ((2, 2), f32),
        ),
        (),
        "outputs",
    )
    shape = (rows, half_states, columns)
    return (image_two.reshape(shape), basis_two.reshape(shape), projected)


def solution(mesh):
    return jax.shard_map(
        per_device,
        mesh=mesh,
        in_specs=(
            P(("groups", "brow"), None, "bcol"),
            P(("groups", "mpo"), "brow", None),
            P("groups", "bcol", None),
            P(),
            P(),
            P("groups"),
        ),
        out_specs=(
            P(("groups", "brow"), "mpo", "bcol"),
            P(("groups", "brow"), "mpo", "bcol"),
            P("groups", None),
        ),
        check_vma=False,
    )
```

```python
import jax
import jax.numpy as jnp
from jax import lax
from jax.experimental import pallas as pl
from jax.experimental.pallas import tpu as pltpu
from jax.sharding import PartitionSpec as P

EPSILON = 1e-06
SHRINK = 2.0**-12
GROW = 1.0 / SHRINK
SLOT = 32
LOCAL = 4
GROUP = 16
VMEM_LIMIT = 40 * 2**20
SHORT = pl.CostEstimate(flops=10**9, bytes_accessed=2**21, transcendentals=0)
WHOLE = pl.BlockSpec(memory_space=pltpu.VMEM)


def swap_cores(x):
    return lax.ppermute(x, "mpo", [(0, 1), (1, 0)])


def partner_of(block, slab, core, odd):
    blocks, slabs = lax.axis_size("brow"), lax.axis_size("bcol")
    other = (block + 1 if block % 2 else block - 1) if odd[core] else block ^ 1
    if 0 <= other < blocks:
        return other, slab, core
    if odd[0] == odd[1]:
        return block, slab, 1 - core
    return block, slab ^ 1 if slab ^ 1 < slabs else slab, core


def place_of(block, slab, core):
    return (block * lax.axis_size("bcol") + slab) * 2 + core


def trade(x, odd):
    pairs = []
    for block in range(lax.axis_size("brow")):
        for slab in range(lax.axis_size("bcol")):
            for core in range(2):
                other = partner_of(block, slab, core, odd)
                pairs.append((place_of(block, slab, core), place_of(*other)))
    return lax.ppermute(x, ("brow", "bcol", "mpo"), pairs)


def halo_places(rows):
    even = lax.rem(lax.axis_index("brow") + lax.axis_index("mpo"), 2) == 0
    direct = jnp.where(even, 2 * rows, 0)
    return pl.multiple_of(direct, rows), pl.multiple_of(2 * rows - direct, rows)


def states_apart(wide, rows, states, store):
    lanes = wide.shape[1]
    for state in range(states):
        piece = wide[pl.ds(state, rows, stride=states), :].astype(jnp.bfloat16)
        store(slice(state * lanes, (state + 1) * lanes), piece)


def prepare_kernel(
    env_mine, env_there, mask, both_mpo,
    env_one, env_two, coupling,
    env, by_bond, left_pad, right_pad, left_rows, right_rows, spread,
):
    core = lax.axis_index("mpo")
    share, rows, _ = env_mine.shape
    half = rows // 2
    here = pl.ds(pl.multiple_of(core * half, half), half)
    part = SLOT // 2
    used, bonds = both_mpo.shape[0] // 2, both_mpo.shape[1]
    states = used // bonds
    left_pad[...] = jnp.zeros_like(left_pad)
    right_pad[...] = jnp.zeros_like(right_pad)
    left_pad[0:used, 0:bonds] = both_mpo[0:used, :]
    right_pad[0:used, 0:bonds] = both_mpo[used : 2 * used, :]
    for state in range(states):
        for group, owner in enumerate((core, 1 - core)):
            start = state * SLOT + group * part
            left_rows[start : start + part, :] = left_pad[
                pl.ds(owner * (share * states) + state, part, stride=states), :
            ]
        across = right_pad[pl.ds(state, SLOT, stride=states), :]
        right_rows[state * SLOT : (state + 1) * SLOT, :] = jnp.transpose(across)[0:SLOT, :]
    joined = lax.dot_general(
        right_rows[...],
        left_rows[:, 0:SLOT],
        (((1,), (1,)), ((), ())),
        precision=lax.Precision.HIGHEST,
        preferred_element_type=jnp.float32,
    )
    width = LOCAL * SLOT
    for i in range(LOCAL):
        for j in range(LOCAL):
            for inner in range(LOCAL):
                start = inner * SLOT * states + i * LOCAL + j
                spread[pl.ds(start, SLOT, stride=states), :] = joined[
                    (j * LOCAL + inner) * SLOT : (j * LOCAL + inner + 1) * SLOT,
                    i * width : (i + 1) * width,
                ]
    for inner in range(LOCAL):
        start = inner * SLOT * states
        coupling[:, inner * width : (inner + 1) * width] = spread[
            start : start + used, :
        ].astype(jnp.bfloat16)

    band = mask.shape[1]
    by_bond[...] = jnp.zeros_like(by_bond)
    for low in range(0, band, 128):
        width = min(128, band - low)
        base = low // 128 * SLOT * half
        for group, source in enumerate((env_mine, env_there)):
            for bond in range(share):
                start = base + (group * part + bond) * half
                piece = source[bond, here, low : low + width].astype(jnp.float32)
                by_bond[start : start + half, 0:width] = piece
        for row in range(half):
            piece = by_bond[pl.ds(base + row, SLOT, stride=half), :][:, 0:width]
            kept = jnp.where(mask[row : row + 1, low : low + width] > 0.0, piece, 0.0)
            env[row * SLOT : (row + 1) * SLOT, low : low + width] = kept.astype(jnp.bfloat16)

    direct, passed = halo_places(rows)
    even = lax.rem(lax.axis_index("brow"), 2) == 0
    above, below = jnp.where(even, 2 * rows, 0), jnp.where(even, 0, 2 * rows)
    shares = [base + share * half for base in (rows, above, below) for share in (core, 1 - core)]
    for target, starts in ((env_one, (rows, direct, passed)), (env_two, shares)):
        size = band // len(starts)
        taken = lax.broadcasted_iota(jnp.int32, (band, band), 0)
        place = lax.broadcasted_iota(jnp.int32, (band, band), 1)
        chosen = jnp.zeros((band, band), jnp.bool_)
        for index, start in enumerate(starts):
            inside = (place >= index * size) & (place < (index + 1) * size)
            chosen = chosen | (inside & (taken == place + (start - index * size)))
        order = jnp.where(chosen, 1.0, 0.0).astype(jnp.bfloat16)
        moved = jnp.dot(env[...], order, preferred_element_type=jnp.float32)
        target[...] = moved.astype(jnp.bfloat16)


def apply_steps(env, coupling, right, pieces, contracted, mixed, image):
    groups, depth, width = contracted.shape
    lanes = right.shape[1]
    group = width // lanes
    states = depth // SLOT
    bonds = mixed.shape[1] // lanes
    extended = jnp.concatenate([piece[...] for piece in pieces], axis=0)
    product = jnp.dot(env[...], extended, preferred_element_type=jnp.float32)
    product = product.astype(jnp.bfloat16)
    for state in range(states):
        place = state % LOCAL * LOCAL + state // LOCAL
        for row in range(groups * group):
            contracted[
                row // group,
                place * SLOT : (place + 1) * SLOT,
                row % group * lanes : (row % group + 1) * lanes,
            ] = product[row * SLOT : (row + 1) * SLOT, state * lanes : (state + 1) * lanes]

    def mix(step):
        product = jnp.dot(coupling[...], contracted[step], preferred_element_type=jnp.float32)
        product = product.astype(jnp.bfloat16)
        for part in range(group):
            start = (group * step + part) * states
            for bond in range(bonds):
                mixed[start : start + states, bond * lanes : (bond + 1) * lanes] = product[
                    bond * states : (bond + 1) * states, part * lanes : (part + 1) * lanes
                ]

    def finish(step):
        place = slice(group * step * states, group * (step + 1) * states)
        image[place, :] = SHRINK * jnp.dot(
            mixed[place, :], right[...], preferred_element_type=jnp.float32
        )

    mix(0)
    for step in range(groups):
        if step + 1 < groups:
            mix(step + 1)
        finish(step)


def column_sum(x):
    return jnp.sum(x, axis=0, keepdims=True)


def state_half(image, states, index):
    pieces = image.reshape(image.shape[0] // states, states, image.shape[1])
    return jnp.where(index == 0, pieces[:, : states // 2, :], pieces[:, states // 2 :, :])


def lay_kernel(vector, direct, vector_rows, direct_rows, wide):
    rows, width = vector_rows.shape
    states = width // vector.shape[1]
    for source, target in ((vector, vector_rows), (direct, direct_rows)):
        wide[...] = source[...].astype(jnp.float32)

        def store(columns, piece, target=target):
            target[:, columns] = piece

        states_apart(wide, rows, states, store)


def first_kernel(
    env, coupling, right, vector_rows, direct_rows, passed_in,
    image, image_rows,
    wide, passed_rows, contracted, mixed,
):
    rows = vector_rows.shape[0]
    states = passed_in.shape[0] // rows
    half = image.shape[0]
    wide[...] = passed_in[...].astype(jnp.float32)

    def store(columns, piece):
        passed_rows[:, columns] = piece

    states_apart(wide, rows, states, store)
    pieces = (vector_rows, direct_rows, passed_rows)
    apply_steps(env, coupling, right, pieces, contracted, mixed, image)

    def store_rows(columns, piece):
        image_rows[:, columns] = piece

    states_apart(image, half // states, states, store_rows)


def sums_kernel(image, vector, sums):
    half, lanes = image.shape
    start = pl.multiple_of(lax.axis_index("mpo") * half, half)
    own = vector[pl.ds(start, half), :].astype(jnp.float32)
    out = image[...]
    sums[...] = jnp.concatenate(
        [column_sum(own * own), column_sum(own * out), column_sum(out * out)]
        + [jnp.zeros((5, lanes), jnp.float32)],
        axis=0,
    )


def second_kernel(
    env, coupling, right, own_here, own_there, even_here, even_there, odd_here, odd_there,
    first, vector, sums,
    image, sent, totals,
    contracted, mixed,
):
    part = own_here.shape[0]
    half = first.shape[0]
    core = lax.axis_index("mpo")
    pieces = (own_here, own_there, even_here, even_there, odd_here, odd_there)
    apply_steps(env, coupling, right, pieces, contracted, mixed, image)
    out = image[...]
    states = half // part
    sent[0:part] = state_half(first[...], states, 1 - core)
    sent[part : 2 * part] = state_half(out, states, 1 - core)
    own = vector[pl.ds(pl.multiple_of(core * half, half), half), :].astype(jnp.float32)
    lanes = out.shape[1]
    columns = jnp.concatenate(
        [sums[0:3, :], column_sum(own * out), column_sum(first[...] * out)]
        + [jnp.zeros((3, lanes), jnp.float32)],
        axis=0,
    )
    lane = lax.broadcasted_iota(jnp.int32, columns.shape, 1)
    row = lax.broadcasted_iota(jnp.int32, columns.shape, 0)
    spread = jnp.where(lane == row, jnp.sum(columns, axis=1, keepdims=True), 0.0)
    totals[...] = jnp.broadcast_to(column_sum(spread)[None], totals.shape)


def final_kernel(
    entries, first, second, got, vector, gathered,
    image_two, basis_two, projected,
):
    half = got.shape[0] // 2
    half_states = got.shape[1]
    states = 2 * half_states
    lanes = first.shape[1]
    core = lax.axis_index("mpo")
    totals = jnp.sum(gathered[...], axis=0)
    lane = lax.broadcasted_iota(jnp.int32, totals.shape, 1)
    s_aa, s_ay, s_yy, s_az, s_yz = (
        jnp.sum(jnp.where(lane == i, totals, 0.0), axis=1, keepdims=True) for i in range(5)
    )
    scale_sq = s_aa / entries + EPSILON
    shrunk = s_ay / entries / scale_sq
    residual_sq = jnp.maximum(s_yy - 2.0 * shrunk * s_ay + shrunk * shrunk * s_aa, 0.0)
    residual_norm = jnp.sqrt(residual_sq / scale_sq / entries * (GROW * GROW) + EPSILON)
    factor = GROW / (jnp.sqrt(scale_sq) * residual_norm)
    final = (s_yz - shrunk * s_yy - shrunk * s_az + shrunk * shrunk * s_ay) / entries
    gamma = final * factor * factor * GROW
    r = lax.broadcasted_iota(jnp.int32, projected.shape, 0)
    c = lax.broadcasted_iota(jnp.int32, projected.shape, 1)
    diagonal = jnp.where(r == 0, shrunk * GROW, gamma)
    projected[...] = jnp.where(r == c, diagonal, residual_norm)

    size = half * half_states
    own = state_half(vector[...].astype(jnp.float32), states, core).reshape(2 * size, lanes)
    ours = jnp.where(core == 0, own[:size, :], own[size:, :])
    theirs = jnp.where(core == 0, own[size:, :], own[:size, :])
    mine = [state_half(image[...], states, core) for image in (first, second)]
    for index, (y, z), a in (
        (core, mine, ours),
        (1 - core, (got[0:half], got[half : 2 * half]), theirs),
    ):
        y = y.reshape(size, lanes)
        z = z.reshape(size, lanes)
        place = pl.ds(pl.multiple_of(index * size, size), size)
        basis_two[place, :] = ((y - shrunk * a) * factor).astype(jnp.bfloat16)
        image_two[place, :] = ((z - shrunk * y) * (factor * GROW)).astype(jnp.bfloat16)


def call(kernel, operands, outs, scratch, name, cost=None):
    return pl.pallas_call(
        kernel,
        out_shape=tuple(jax.ShapeDtypeStruct(shape, dtype) for shape, dtype in outs),
        in_specs=[WHOLE] * len(operands),
        out_specs=(WHOLE,) * len(outs),
        scratch_shapes=[pltpu.VMEM(shape, dtype) for shape, dtype in scratch],
        cost_estimate=cost,
        compiler_params=pltpu.CompilerParams(vmem_limit_bytes=VMEM_LIMIT),
        name=name,
    )(*operands)


def per_device(amplitudes, left_env, right_env, mpo_left, mpo_right, sector_table):
    rows, states, columns = amplitudes.shape
    band = left_env.shape[2]
    bonds = mpo_left.shape[0]
    half = rows // 2
    half_states = states // 2
    size = half * states
    block = lax.axis_index("brow")
    core = lax.axis_index("mpo")
    axes = ("brow", "bcol", "mpo")
    peers = lax.axis_size(axes)
    entries = float(rows * lax.axis_size("brow") * states * columns * lax.axis_size("bcol"))
    f32, bf16 = jnp.float32, jnp.bfloat16
    flat = amplitudes.reshape(rows * states, columns)

    env_there = swap_cores(left_env)
    direct_one = trade(flat, (False, True))

    outside = jnp.full((rows,), -1, dtype=jnp.int32)
    padded = jnp.concatenate([outside, sector_table, outside])
    own_labels = lax.dynamic_slice_in_dim(padded, (block + 1) * rows + core * half, half, 0)
    partner = lax.dynamic_slice_in_dim(padded, block * rows, 3 * rows, 0)
    mask = (own_labels[:, None] == partner[None, :]).astype(f32)
    both = jnp.concatenate([mpo_left, mpo_right], axis=0)
    both = jnp.transpose(both, (0, 2, 3, 1)).reshape(2 * bonds * states, bonds)
    env_one, env_two, coupling = call(
        prepare_kernel,
        (left_env, env_there, mask, both),
        (
            ((half * SLOT, band), bf16),
            ((half * SLOT, band), bf16),
            ((bonds * states, states * SLOT), bf16),
        ),
        (
            ((half * SLOT, band), bf16),
            ((-(-band // 128) * SLOT * half, 128), f32),
            ((SLOT * states, 128), f32),
            ((SLOT * states, 128), f32),
            ((states * SLOT, 128), f32),
            ((states * SLOT, SLOT), f32),
            ((states // LOCAL * SLOT * states, 128), f32),
        ),
        "operands",
        cost=pl.CostEstimate(flops=4 * 10**9, bytes_accessed=2**23, transcendentals=0),
    )
    direct_one, env_one, coupling = lax.optimization_barrier((direct_one, env_one, coupling))
    passed_one = swap_cores(direct_one)
    right = right_env.reshape(bonds * columns, columns)

    work = (
        ((half // GROUP, states * SLOT, GROUP * columns), bf16),
        ((size, bonds * columns), bf16),
    )
    laid = ((rows, states * columns), bf16)
    wide = ((rows * states, columns), f32)
    vector_rows, direct_rows = call(
        lay_kernel, (flat, direct_one), (laid, laid), (wide,), "rows", cost=SHORT
    )
    first, first_rows = call(
        first_kernel,
        (env_one, coupling, right, vector_rows, direct_rows, passed_one),
        (((size, columns), f32), ((half, states * columns), bf16)),
        (wide, laid) + work,
        "first_image",
    )
    (sums,) = call(sums_kernel, (first, flat), (((8, columns), f32),), (), "sums", cost=SHORT)

    even_rows = trade(first_rows, (False, False))
    odd_rows = trade(first_rows, (True, True))
    pieces = [(x, swap_cores(x)) for x in (first_rows, even_rows, odd_rows)]
    pieces = [x for pair in pieces for x in pair]

    second, sent, totals = call(
        second_kernel,
        (env_two, coupling, right, *pieces, first, flat, sums),
        (
            ((size, columns), f32),
            ((2 * half, half_states, columns), f32),
            ((peers, 1, columns), f32),
        ),
        work,
        "second_image",
    )
    got = swap_cores(sent)
    gathered = lax.all_to_all(totals, axes, 0, 0)

    def finish(*refs):
        final_kernel(entries, *refs)

    image_two, basis_two, projected = call(
        finish,
        (first, second, got, flat, gathered),
        (
            ((rows * half_states, columns), bf16),
            ((rows * half_states, columns), bf16),
            ((2, 2), f32),
        ),
        (),
        "outputs",
    )
    shape = (rows, half_states, columns)
    return (image_two.reshape(shape), basis_two.reshape(shape), projected)


def solution(mesh):
    return jax.shard_map(
        per_device,
        mesh=mesh,
        in_specs=(
            P(("groups", "brow"), None, "bcol"),
            P(("groups", "mpo"), "brow", None),
            P("groups", "bcol", None),
            P(),
            P(),
            P("groups"),
        ),
        out_specs=(
            P(("groups", "brow"), "mpo", "bcol"),
            P(("groups", "brow"), "mpo", "bcol"),
            P("groups", None),
        ),
        check_vma=False,
    )
```
